512 devices in a mesh: pb: 32 (over z_lo, y), ta: 8 (over x, core), row: 2 (over z_hi).
Axes of the slice: x: 4, y: 4, z: 16 (z_hi: 2, z_lo: 8; z = z_hi * 8 + z_lo), core: 2. Of those that a mesh axis runs over, the one named last changes fastest.
Arguments:
- query_features: bfloat16 [16384, 4096], P('pb', 'ta'), may hold values from -6 to 6
- inverse_gram: bfloat16 [4096, 4096], P('pb', 'ta'), may hold values from -0.03125 to 2.03125
- training_features: bfloat16 [8192, 4096], P(('row', 'ta'), 'pb'), parts along dimension 0, may hold values from -0.09375 to 0.09375
- residual_weight: float32 [8192], P(('row', 'ta')), parts along dimension 0, may hold values from 0.05 to 0.95
Outputs:
- scores: float32 [16384, 8192], P('pb', ('row', 'ta')), parts along dimension 1
The draws below stay inside these ranges and needn't reach their ends.
There are 2 independent parts, one for each index of `row`. The reference program is written for one: setup_inputs(seed, part) draws one part's arguments, and reference() takes and returns one part's arrays. A program takes and returns all parts, laid end to end along the dimension named above; an argument that names none is the same for every part. Nothing has to cross between parts.
All inputs are finite; a program needn't handle non-finite values.
Results may differ from the reference program's by a relative error of at most 0.0029.
Values may be sent and summed in bfloat16 or wider, within the bound.
No kernel may reach another device: no remote copies, remote signals or barrier semaphores. Data moves between devices by JAX's collectives and lax.ppermute only.
A program may use at most 64 MiB of HBM per device.

```python
import jax
import jax.numpy as jnp
from jax import lax

P_SIZE = 4096
NQ = 16384
NT = 4096


def draw_inverse_gram(key, part):
    key = jax.random.fold_in(key, 5)
    noise_key, diag_key = jax.random.split(key)
    spread = 0.5 / P_SIZE ** 0.5
    noise = jnp.clip(jax.random.normal(noise_key, (P_SIZE, P_SIZE), jnp.float32), -3.5, 3.5) * spread
    diagonal = jnp.exp(jax.random.uniform(diag_key, (P_SIZE,), jnp.float32, -0.69, 0.69))
    rows_idx = lax.broadcasted_iota(jnp.int32, (P_SIZE, P_SIZE), 0)
    cols_idx = lax.broadcasted_iota(jnp.int32, (P_SIZE, P_SIZE), 1)
    identity = (rows_idx == cols_idx).astype(jnp.float32)
    return (noise + identity * diagonal[:, None]).astype(jnp.bfloat16)


def level_of(stream_key, dims, cuts, smallest, high):
    def one(position, shards_of):
        heights = jax.random.uniform(jax.random.fold_in(jax.random.fold_in(stream_key, 6), position), (shards_of,), jnp.float32, smallest / len(cuts), high / len(cuts))
        return jnp.repeat(jnp.exp(heights), dims[position] // shards_of).reshape((-1,) + (1,) * (len(dims) - position - 1))

    loudness = one(*cuts[0])
    for cut in cuts[1:]:
        loudness = loudness * one(*cut)
    return loudness


def scatter_about(stream_key, extent, width, reach, cuts=(), kind=jnp.bfloat16):
    drawn = jax.random.normal(stream_key, extent, jnp.float32) * width
    if len(cuts) > 0:
        drawn = level_of(stream_key, extent, cuts, -0.22, 0.18) * drawn
    return jnp.clip(drawn, min=-reach, max=reach).astype(kind)


def setup_inputs(seed: int = 0, part: int = 0) -> dict:
    key_of = jax.random.split(jax.random.key(seed), 5)
    part_splits = jax.random.split(jax.random.fold_in(key_of[4], part), 5)
    return {
        "query_features": scatter_about(key_of[0], (NQ, P_SIZE), 1.0, 6.0, ((0, 32), (1, 8))),
        "inverse_gram": draw_inverse_gram(jax.random.fold_in(key_of[4], 71), part),
        "training_features": scatter_about(part_splits[2], (NT, P_SIZE), P_SIZE ** -0.5, 0.09375, ((0, 8), (1, 32))),
        "residual_weight": jnp.clip(0.05 + 0.9 * jax.random.uniform(part_splits[3], (NT,), jnp.float32) ** level_of(part_splits[3], (NT,), ((0, 8),), -0.2, 0.2), 0.05, 0.95),
    }


def reference(query_features, inverse_gram, training_features, residual_weight):
    preconditioned = jnp.dot(query_features, inverse_gram, preferred_element_type=jnp.float32).astype(jnp.bfloat16)
    raw = jnp.dot(preconditioned, training_features.T, preferred_element_type=jnp.float32)
    return raw * residual_weight[None, :]
```

```python
import jax
import jax.numpy as jnp
from jax import lax
from jax.experimental import pallas as pl
from jax.experimental.pallas import tpu as pltpu
from jax.sharding import Mesh, PartitionSpec as P

NT_DIMS = (((1,), (1,)), ((), ()))
RELATIVE = (0, 4, 2, 6, 1, 5, 3, 7)


def product_kernel(slots, place, left_ref, right_ref, out_ref, total):
    step = pl.program_id(0)

    @pl.when(step == 0)
    def _():
        total[...] = jnp.zeros_like(total)

    total[...] += lax.dot_general(
        left_ref[0], right_ref[0], NT_DIMS, preferred_element_type=jnp.float32
    )

    @pl.when(step == pl.num_programs(0) - 1)
    def _():
        out_ref[...] = total[...].astype(out_ref.dtype)


def kernel_matrix(slots, inverse_gram, training):
    n, t, depth = training.shape
    rows = inverse_gram.shape[1]
    return pl.pallas_call(
        lambda s, *refs: product_kernel(s, None, *refs),
        out_shape=jax.ShapeDtypeStruct((rows, t), jnp.bfloat16),
        grid_spec=pltpu.PrefetchScalarGridSpec(
            num_scalar_prefetch=1,
            grid=(n,),
            in_specs=[
                pl.BlockSpec((1, rows, depth), lambda s, slots: (slots[s], 0, 0)),
                pl.BlockSpec((1, t, depth), lambda s, slots: (s, 0, 0)),
            ],
            out_specs=pl.BlockSpec((rows, t), lambda s, slots: (0, 0)),
            scratch_shapes=[pltpu.VMEM((rows, t), jnp.float32)],
        ),
        compiler_params=pltpu.CompilerParams(vmem_limit_bytes=24 * 1024 * 1024),
        cost_estimate=pl.CostEstimate(
            flops=2 * n * rows * t * depth, bytes_accessed=2 * n * depth * (rows + t), transcendentals=0
        ),
        name="kernel_matrix",
    )(slots, inverse_gram, training)


def score_columns(slots, place, query, parts, weight, out, columns):
    n, rows, depth = query.shape
    t = parts[0].shape[2]
    each = n // len(parts)

    def kernel(slots, place, query_ref, *refs):
        part_refs, weight_ref, out_ref, total = refs[: len(parts)], refs[len(parts)], refs[-2], refs[-1]
        step = pl.program_id(0)

        @pl.when(step == 0)
        def _():
            total[...] = jnp.zeros_like(total)

        for k, part_ref in enumerate(part_refs):

            @pl.when(step // each == k)
            def _():
                total[...] += jnp.dot(query_ref[0], part_ref[0], preferred_element_type=jnp.float32)

        @pl.when(step == n - 1)
        def _():
            out_ref[...] = total[...] * weight_ref[...]

    operands = [slots, place, query, *parts, weight] + ([] if out is None else [out])
    in_specs = [
        pl.BlockSpec((1, rows, depth), lambda s, slots, place: (slots[s], 0, 0)),
        *[
            pl.BlockSpec((1, depth, t), lambda s, slots, place, k=k: (jnp.clip(s - k * each, 0, each - 1), 0, 0))
            for k in range(len(parts))
        ],
        pl.BlockSpec((1, t), lambda s, slots, place: (0, place[0])),
    ]
    if out is not None:
        in_specs.append(pl.BlockSpec(memory_space=pl.ANY))
    return pl.pallas_call(
        kernel,
        out_shape=jax.ShapeDtypeStruct((rows, columns), jnp.float32),
        grid_spec=pltpu.PrefetchScalarGridSpec(
            num_scalar_prefetch=2,
            grid=(n,),
            in_specs=in_specs,
            out_specs=pl.BlockSpec((rows, t), lambda s, slots, place: (0, place[0])),
            scratch_shapes=[pltpu.VMEM((rows, t), jnp.float32)],
        ),
        input_output_aliases={} if out is None else {len(operands) - 1: 0},
        compiler_params=pltpu.CompilerParams(vmem_limit_bytes=24 * 1024 * 1024),
        cost_estimate=pl.CostEstimate(
            flops=2 * n * rows * t * depth, bytes_accessed=2 * n * depth * (rows + t), transcendentals=0
        ),
        name="score_columns",
    )(*operands)


def gather_z(block):
    held = block[None]
    for distance in (4, 2, 1):
        other = lax.ppermute(held, "z", [(i, i ^ distance) for i in range(8)])
        held = jnp.concatenate([held, other], axis=0)
    return held


def local(query_features, inverse_gram, training_features, residual_weight):
    z, y = lax.axis_index("z"), lax.axis_index("y")
    slots = z ^ jnp.array(RELATIVE, jnp.int32)
    ny = 4

    training = lax.all_to_all(training_features, "y", split_axis=0, concat_axis=1, tiled=True)
    rows = lax.all_gather(inverse_gram, "y", axis=0, tiled=True)
    whole_rows = lax.all_gather(rows, ("x", "core"), axis=0)
    whole_query = lax.all_gather(query_features, ("x", "core"), axis=0)

    whole_training = gather_z(training)
    block = kernel_matrix(slots, whole_rows, whole_training)
    own = gather_z(block)

    up = [(i, (i + 1) % ny) for i in range(ny)]
    down = [(i, (i - 1) % ny) for i in range(ny)]
    below = lax.ppermute(own, "y", up)
    above = lax.ppermute(own, "y", down)
    far_first = lax.ppermute(below[:4], "y", up)
    far_second = lax.ppermute(above[4:], "y", down)

    weight = residual_weight[None, :]
    columns = residual_weight.shape[0]
    out = None
    for distance, parts in ((0, [own]), (ny - 1, [below]), (1, [above]), (2, [far_first, far_second])):
        place = ((y + distance) % ny).astype(jnp.int32)[None]
        out = score_columns(slots, place, whole_query, parts, weight, out, columns)
    return out


def solution(mesh):
    fine = Mesh(mesh.devices.reshape(8, 4, 4, 2, 2), ("z", "y", "x", "core", "row"))
    pb, ta = ("z", "y"), ("x", "core")
    placed = (P(pb, ta), P(pb, ta), P(("row", *ta), pb), P(("row", *ta)))
    return jax.shard_map(
        local, mesh=fine, in_specs=placed, out_specs=P(pb, ("row", *ta)), check_vma=False
    )
```

```python
import jax
import jax.numpy as jnp
from jax import lax
from jax.experimental import pallas as pl
from jax.experimental.pallas import tpu as pltpu
from jax.sharding import Mesh, PartitionSpec as P

NZ, NY, CHUNKS = 8, 4, 2
NT_DIMS = (((1,), (1,)), ((), ()))
RELATIVE = (0, 4, 2, 6, 1, 5, 3, 7)
VMEM_LIMIT = 24 * 1024 * 1024


def kernel_matrix(slots, inverse_gram, training):
    n, t, depth = training.shape
    rows = inverse_gram.shape[1]

    def kernel(slots, gram_ref, training_ref, out_ref, total):
        step = pl.program_id(0)

        @pl.when(step == 0)
        def _():
            total[...] = jnp.zeros_like(total)

        total[...] += lax.dot_general(training_ref[0], gram_ref[0], NT_DIMS, preferred_element_type=jnp.float32)

        @pl.when(step == n - 1)
        def _():
            out_ref[...] = total[...].astype(out_ref.dtype)

    return pl.pallas_call(
        kernel,
        out_shape=jax.ShapeDtypeStruct((t, rows), jnp.bfloat16),
        grid_spec=pltpu.PrefetchScalarGridSpec(
            num_scalar_prefetch=1,
            grid=(n,),
            in_specs=[
                pl.BlockSpec((1, rows, depth), lambda s, slots: (slots[s], 0, 0)),
                pl.BlockSpec((1, t, depth), lambda s, slots: (s, 0, 0)),
            ],
            out_specs=pl.BlockSpec((t, rows), lambda s, slots: (0, 0)),
            scratch_shapes=[pltpu.VMEM((t, rows), jnp.float32)],
        ),
        compiler_params=pltpu.CompilerParams(vmem_limit_bytes=VMEM_LIMIT),
        cost_estimate=pl.CostEstimate(
            flops=2 * n * rows * t * depth, bytes_accessed=2 * n * depth * (rows + t), transcendentals=0
        ),
        name="kernel_matrix",
    )(slots, inverse_gram, training)


def score_columns(slots, place, query, blocks, weight, out, chunk, columns):
    n, rows, depth = query.shape
    ny, _, t, _ = blocks.shape
    width = ny * t

    def kernel(slots, place, query_ref, blocks_ref, weight_ref, *refs):
        out_ref, total = refs[-2:]
        step = pl.program_id(0)

        @pl.when(step == 0)
        def _():
            total[...] = jnp.zeros_like(total)

        ordered = jnp.concatenate([blocks_ref[lax.rem(p - place[0] + ny, ny), 0] for p in range(ny)], axis=0)
        total[...] += lax.dot_general(query_ref[0], ordered, NT_DIMS, preferred_element_type=jnp.float32)

        @pl.when(step == n - 1)
        def _():
            out_ref[...] = total[...] * weight_ref[...]

    operands = [slots, place, query, blocks, weight] + ([] if out is None else [out])
    in_specs = [
        pl.BlockSpec((1, rows, depth), lambda s, slots, place: (slots[s], 0, 0)),
        pl.BlockSpec((ny, 1, t, depth), lambda s, slots, place: (0, s, 0, 0)),
        pl.BlockSpec((1, width), lambda s, slots, place: (0, chunk)),
    ]
    if out is not None:
        in_specs.append(pl.BlockSpec(memory_space=pl.ANY))
    return pl.pallas_call(
        kernel,
        out_shape=jax.ShapeDtypeStruct((rows, columns), jnp.float32),
        grid_spec=pltpu.PrefetchScalarGridSpec(
            num_scalar_prefetch=2,
            grid=(n,),
            in_specs=in_specs,
            out_specs=pl.BlockSpec((rows, width), lambda s, slots, place: (0, chunk)),
            scratch_shapes=[pltpu.VMEM((rows, width), jnp.float32)],
        ),
        input_output_aliases={} if out is None else {len(operands) - 1: 0},
        compiler_params=pltpu.CompilerParams(vmem_limit_bytes=VMEM_LIMIT),
        cost_estimate=pl.CostEstimate(
            flops=2 * n * rows * width * depth, bytes_accessed=2 * n * depth * (rows + width), transcendentals=0
        ),
        name="score_columns",
    )(*operands)


def exchange(held, distance):
    other = lax.ppermute(held, "z", [(i, i ^ distance) for i in range(NZ)])
    return jnp.concatenate([held, other], axis=0)


def gather_y(own):
    up = [(i, (i + 1) % NY) for i in range(NY)]
    down = [(i, (i - 1) % NY) for i in range(NY)]
    half = own.shape[0] // 2
    below = lax.ppermute(own, "y", up)
    above = lax.ppermute(own, "y", down)
    far = jnp.concatenate(
        [lax.ppermute(below[:half], "y", up), lax.ppermute(above[half:], "y", down)], axis=0
    )
    return jnp.stack([own, above, far, below])


def local(query_features, inverse_gram, training_features, residual_weight):
    slots = lax.axis_index("z") ^ jnp.array(RELATIVE, jnp.int32)
    place = lax.axis_index("y").astype(jnp.int32)[None]
    columns, lanes = training_features.shape
    rows, depth = inverse_gram.shape
    t = columns // (CHUNKS * NY)

    gram_tiles = inverse_gram.reshape(rows, NY, lanes).transpose(1, 0, 2).reshape(NY * rows, lanes)
    pieces = training_features.reshape(CHUNKS, NY, t, lanes).transpose(1, 0, 2, 3).reshape(NY, CHUNKS * t, lanes)
    sent = jnp.concatenate([pieces, jnp.broadcast_to(gram_tiles, (NY, *gram_tiles.shape))], axis=1)
    got = lax.all_to_all(sent, "y", split_axis=0, concat_axis=0, tiled=True)
    training = got[:, : CHUNKS * t].reshape(NY, CHUNKS, t, lanes).transpose(1, 2, 0, 3).reshape(CHUNKS, t, NY * lanes)
    gram_rows = got[:, CHUNKS * t :].reshape(NY, NY, rows, lanes).transpose(0, 2, 1, 3).reshape(NY * rows, depth)

    gram = lax.all_gather(gram_rows, ("x", "core"), axis=0)
    query = lax.all_gather(query_features, ("x", "core"), axis=0)

    weight = residual_weight[None, :]
    held = [training[c][None] for c in range(CHUNKS)]
    for distance in (4, 2, 1):
        held = [exchange(h, distance) for h in held]
    held = [kernel_matrix(slots, gram, h)[None] for h in held]
    for distance in (4, 2, 1):
        held = [exchange(h, distance) for h in held]
    out = None
    for c, h in enumerate(held):
        out = score_columns(slots, place, query, gather_y(h), weight, out, c, columns)
    return out


def solution(mesh):
    fine = Mesh(mesh.devices.reshape(NZ, NY, 4, 2, 2), ("z", "y", "x", "core", "row"))
    pb, ta = ("z", "y"), ("x", "core")
    placed = (P(pb, ta), P(pb, ta), P(("row", *ta), pb), P(("row", *ta)))
    return jax.shard_map(
        local, mesh=fine, in_specs=placed, out_specs=P(pb, ("row", *ta)), check_vma=False
    )
```

```python
import jax
import jax.numpy as jnp
from jax import lax
from jax.experimental import pallas as pl
from jax.experimental.pallas import tpu as pltpu
from jax.sharding import Mesh, PartitionSpec as P

NZ, NY, CHUNKS = 8, 4, 2
NT_DIMS = (((1,), (1,)), ((), ()))
RELATIVE = (0, 4, 2, 6, 1, 5, 3, 7)
VMEM_LIMIT = 57 * 1024 * 1024


def kernel_matrix(slots, gram, training):
    n, t, depth = training.shape
    rows = gram.shape[1]

    def kernel(slots, gram_ref, training_ref, out_ref, held, arrived):
        copies = [pltpu.make_async_copy(gram_ref.at[slots[s]], held.at[s], arrived.at[s]) for s in range(n)]
        for copy in copies:
            copy.start()
        total = jnp.zeros((t, rows), jnp.float32)
        for s, copy in enumerate(copies):
            copy.wait()
            total += lax.dot_general(training_ref[s], held[s], NT_DIMS, preferred_element_type=jnp.float32)
        out_ref[...] = total.astype(out_ref.dtype)

    return pl.pallas_call(
        kernel,
        out_shape=jax.ShapeDtypeStruct((t, rows), jnp.bfloat16),
        in_specs=[
            pl.BlockSpec(memory_space=pltpu.SMEM),
            pl.BlockSpec(memory_space=pltpu.HBM),
            pl.BlockSpec(memory_space=pltpu.VMEM),
        ],
        out_specs=pl.BlockSpec(memory_space=pltpu.VMEM),
        scratch_shapes=[pltpu.VMEM((n, rows, depth), jnp.bfloat16), pltpu.SemaphoreType.DMA((n,))],
        compiler_params=pltpu.CompilerParams(vmem_limit_bytes=VMEM_LIMIT),
        cost_estimate=pl.CostEstimate(
            flops=2 * n * rows * t * depth, bytes_accessed=2 * n * depth * (rows + t), transcendentals=0
        ),
        name="kernel_matrix",
    )(slots, gram, training)


def score_columns(slots, place, query, blocks, weight, out, chunk):
    n, rows, depth = query.shape
    t = blocks[0][0].shape[1]
    width = NY * t
    columns = weight.shape[1]
    parts = [(d, part) for d, cut in enumerate(blocks) for part in cut]

    def kernel(slots, place, query_ref, weight_ref, *refs):
        part_refs = refs[: len(parts)]
        out_ref, held, ordered, total, query_sems, part_sems = refs[-6:]
        part_copies, first = [], 0
        for k, ((d, part), ref) in enumerate(zip(parts, part_refs)):
            size = part.shape[0]
            target = ordered.at[pl.ds(first, size), lax.rem(place[0] + d, NY)]
            part_copies.append(pltpu.make_async_copy(ref, target, part_sems.at[k]))
            first = (first + size) % n
        copies = [pltpu.make_async_copy(query_ref.at[slots[s]], held.at[s], query_sems.at[s]) for s in range(n)]
        for copy in part_copies + copies:
            copy.start()
        for copy in part_copies:
            copy.wait()
        for s, copy in enumerate(copies):
            copy.wait()
            product = lax.dot_general(
                held[s], ordered[s].reshape(width, depth), NT_DIMS, preferred_element_type=jnp.float32
            )
            if s == 0:
                total[...] = product
            elif s < n - 1:
                total[...] += product
            else:
                out_ref[...] = (total[...] + product) * weight_ref[...]

    operands = [slots, place, query, weight, *(part for _, part in parts)] + ([] if out is None else [out])
    in_specs = [
        pl.BlockSpec(memory_space=pltpu.SMEM),
        pl.BlockSpec(memory_space=pltpu.SMEM),
        pl.BlockSpec(memory_space=pltpu.HBM),
        pl.BlockSpec((1, width), lambda _: (0, chunk)),
    ] + [pl.BlockSpec(memory_space=pl.ANY)] * (len(operands) - 4)
    return pl.pallas_call(
        kernel,
        out_shape=jax.ShapeDtypeStruct((rows, columns), jnp.float32),
        grid=(1,),
        in_specs=in_specs,
        out_specs=pl.BlockSpec((rows, width), lambda _: (0, chunk)),
        scratch_shapes=[
            pltpu.VMEM((n, rows, depth), jnp.bfloat16),
            pltpu.VMEM((n, NY, t, depth), jnp.bfloat16),
            pltpu.VMEM((rows, width), jnp.float32),
            pltpu.SemaphoreType.DMA((n,)),
            pltpu.SemaphoreType.DMA((len(parts),)),
        ],
        input_output_aliases={} if out is None else {len(operands) - 1: 0},
        compiler_params=pltpu.CompilerParams(vmem_limit_bytes=VMEM_LIMIT),
        cost_estimate=pl.CostEstimate(
            flops=2 * n * rows * width * depth, bytes_accessed=2 * n * depth * (rows + width), transcendentals=0
        ),
        name="score_columns",
    )(*operands)


def after(array, *earlier):
    return lax.optimization_barrier((array, earlier))[0]


def exchange(held, distance):
    other = lax.ppermute(held, "z", [(i, i ^ distance) for i in range(NZ)])
    return jnp.concatenate([held, other], axis=0)


UP = [(i, (i + 1) % NY) for i in range(NY)]
DOWN = [(i, (i - 1) % NY) for i in range(NY)]


def local(query_features, inverse_gram, training_features, residual_weight):
    slots = lax.axis_index("z") ^ jnp.array(RELATIVE, jnp.int32)
    place = lax.axis_index("y").astype(jnp.int32)[None]
    columns, lanes = training_features.shape
    rows, depth = inverse_gram.shape
    t = columns // (CHUNKS * NY)

    gram_tiles = inverse_gram.reshape(rows, NY, lanes).transpose(1, 0, 2).reshape(NY * rows, lanes)
    pieces = training_features.reshape(CHUNKS, NY, t, lanes).transpose(1, 0, 2, 3).reshape(NY, CHUNKS * t, lanes)
    sent = jnp.concatenate([pieces, jnp.broadcast_to(gram_tiles, (NY, *gram_tiles.shape))], axis=1)
    got = lax.all_to_all(sent, "y", split_axis=0, concat_axis=0, tiled=True)
    training = got[:, : CHUNKS * t].reshape(NY, CHUNKS, t, lanes).transpose(1, 2, 0, 3).reshape(CHUNKS, t, NY * lanes)
    gram_rows = got[:, CHUNKS * t :].reshape(NY, NY, rows, lanes).transpose(0, 2, 1, 3).reshape(NY * rows, depth)

    gram = lax.all_gather(gram_rows, ("x", "core"), axis=0)
    query = lax.all_gather(after(query_features, gram_rows), ("x", "core"), axis=0)
    weight = residual_weight[None, :]

    a, b = training[0][None], training[1][None]
    for distance in (4, 2, 1):
        a, b = exchange(a, distance), exchange(b, distance)
    a, b = kernel_matrix(slots, gram, a)[None], kernel_matrix(slots, gram, b)[None]

    a = exchange(exchange(a, 4), 2)
    b = after(b, a)
    a = exchange(a, 1)
    b = exchange(b, 4)
    half = NZ // 2
    below, above = lax.ppermute(a, "y", UP), lax.ppermute(a, "y", DOWN)
    b = exchange(b, 2)
    b = exchange(b, 1)
    far = lax.ppermute(below[:half], "y", UP), lax.ppermute(above[half:], "y", DOWN)
    b = after(b, below, above)
    below_b, above_b = lax.ppermute(b, "y", UP), lax.ppermute(b, "y", DOWN)
    out = score_columns(slots, place, query, ((a,), (above,), far, (below,)), weight, None, 0)
    first, second = after(below_b[:half], out), after(above_b[half:], out)
    far_b = lax.ppermute(first, "y", UP), lax.ppermute(second, "y", DOWN)
    return score_columns(slots, place, query, ((b,), (above_b,), far_b, (below_b,)), weight, out, 1)


def solution(mesh):
    fine = Mesh(mesh.devices.reshape(NZ, NY, 4, 2, 2), ("z", "y", "x", "core", "row"))
    pb, ta = ("z", "y"), ("x", "core")
    placed = (P(pb, ta), P(pb, ta), P(("row", *ta), pb), P(("row", *ta)))
    return jax.shard_map(
        local, mesh=fine, in_specs=placed, out_specs=P(pb, ("row", *ta)), check_vma=False
    )
```

```python
import jax
import jax.numpy as jnp
from jax import lax
from jax.experimental import pallas as pl
from jax.experimental.pallas import tpu as pltpu
from jax.sharding import Mesh, PartitionSpec as P

NZ, NY, HALVES = 8, 4, 2
NN_DIMS = (((1,), (0,)), ((), ()))
NT_DIMS = (((1,), (1,)), ((), ()))
RELATIVE = (0, 4, 2, 6, 1, 5, 3, 7)
VMEM_LIMIT = 24 * 1024 * 1024


def product(slots, place, left, blocks, dims, half, start=None, weight=None, out=None, dtype=jnp.float32):
    n, rows, depth = left.shape
    width = depth // NY
    columns = blocks[0][1][0].shape[2 if dims == NN_DIMS else 1]
    row_block = 0
    if half is not None and weight is None:
        rows, row_block = rows // HALVES, half
    operands = [slots, place, left]
    in_specs = [pl.BlockSpec((1, rows, depth), lambda s, slots, place: (slots[s], row_block, 0))]
    for _, cuts in blocks:
        first = 0
        for cut in cuts:
            size, *block = cut.shape
            in_specs.append(
                pl.BlockSpec(
                    (1, *block),
                    lambda s, slots, place, first=first, size=size: (jnp.clip(s - first, 0, size - 1), 0, 0),
                )
            )
            operands.append(cut)
            first += size
    if start is not None:
        in_specs.append(pl.BlockSpec((rows, columns), lambda s, slots, place: (row_block, 0)))
        operands.append(start)
    if weight is not None:
        in_specs.append(pl.BlockSpec((1, columns), lambda s, slots, place: (0, 0)))
        operands.append(weight)
    aliases = {}
    if out is not None:
        in_specs.append(pl.BlockSpec(memory_space=pl.ANY))
        aliases = {len(operands): 0}
        operands.append(out)

    def kernel(slots, place, left_ref, *refs):
        refs = list(refs)
        out_ref, total = refs[-2:]
        step = pl.program_id(0)
        cut_refs = [(d, [refs.pop(0) for _ in cuts]) for d, cuts in blocks]
        start_ref = refs.pop(0) if start is not None else None
        weight_ref = refs.pop(0) if weight is not None else None

        @pl.when(step == 0)
        def _():
            total[...] = jnp.zeros_like(total) if start_ref is None else start_ref[...]

        for d, cut in cut_refs:
            offset = pl.multiple_of(lax.rem(place[0] + d, NY) * width, width)
            right = cut[0][0] if len(cut) == 1 else jnp.where(step < n // 2, cut[0][0], cut[1][0])
            total[...] += lax.dot_general(
                left_ref[0, :, pl.ds(offset, width)], right, dims, preferred_element_type=jnp.float32
            )

        @pl.when(step == n - 1)
        def _():
            whole = total[...] if weight_ref is None else total[...] * weight_ref[...]
            out_ref[...] = whole.astype(out_ref.dtype)

    whole_out = weight is not None
    return pl.pallas_call(
        kernel,
        out_shape=jax.ShapeDtypeStruct((rows * HALVES if whole_out else rows, columns), dtype),
        grid_spec=pltpu.PrefetchScalarGridSpec(
            num_scalar_prefetch=2,
            grid=(n,),
            in_specs=in_specs,
            out_specs=pl.BlockSpec((rows, columns), lambda s, slots, place: (half if whole_out else 0, 0)),
            scratch_shapes=[pltpu.VMEM((rows, columns), jnp.float32)],
        ),
        input_output_aliases=aliases,
        compiler_params=pltpu.CompilerParams(vmem_limit_bytes=VMEM_LIMIT),
        cost_estimate=pl.CostEstimate(
            flops=2 * n * rows * columns * width * len(blocks),
            bytes_accessed=2 * n * (rows * depth + columns * width * len(blocks)),
            transcendentals=0,
        ),
        name="scores" if whole_out else "preconditioned",
    )(*operands)


def after(array, *earlier):
    return lax.optimization_barrier((array, earlier))[0]


def exchange(held, distance):
    other = lax.ppermute(held, "z", [(i, i ^ distance) for i in range(NZ)])
    return jnp.concatenate([held, other], axis=0)


def neighbours_y(own):
    return (
        lax.ppermute(own, "y", [(i, (i + 1) % NY) for i in range(NY)]),
        lax.ppermute(own, "y", [(i, (i - 1) % NY) for i in range(NY)]),
    )


def opposite_y(below, above):
    half = below.shape[0] // 2
    return (
        lax.ppermute(below[:half], "y", [(i, (i + 1) % NY) for i in range(NY)]),
        lax.ppermute(above[half:], "y", [(i, (i - 1) % NY) for i in range(NY)]),
    )


def local(query_features, inverse_gram, training_features, residual_weight):
    slots = lax.axis_index("z") ^ jnp.array(RELATIVE, jnp.int32)
    place = lax.axis_index("y").astype(jnp.int32)[None]
    ta = ("x", "core")

    query = lax.all_gather(query_features, ta, axis=0)
    gram = exchange(exchange(exchange(inverse_gram[None], 4), 2), 1)
    gram_below, gram_above = neighbours_y(gram)
    training = exchange(after(training_features[None], gram), 4)
    gram_far = opposite_y(after(gram_below, training), after(gram_above, training))
    training = exchange(training, 2)
    query = after(query, training)
    training = exchange(training, 1)
    near = product(
        slots, place, query, ((0, (gram,)), (1, (gram_above,)), (3, (gram_below,))), NN_DIMS, None
    )
    gathered = []
    for half in range(HALVES):
        pre = product(slots, place, query, ((2, gram_far),), NN_DIMS, half, start=near, dtype=jnp.bfloat16)
        gathered.append(lax.all_gather(pre, ta, axis=0))

    training = after(training, *gram_far)
    below, above = neighbours_y(training)
    far = opposite_y(below, above)
    weight = residual_weight[None, :]
    out = None
    for half, pre in enumerate(gathered):
        blocks = ((0, (training,)), (1, (above,)), (2, far), (3, (below,)))
        out = product(slots, place, pre, blocks, NT_DIMS, half, weight=weight, out=out)
    return out


def solution(mesh):
    fine = Mesh(mesh.devices.reshape(NZ, NY, 4, 2, 2), ("z", "y", "x", "core", "row"))
    pb, ta = ("z", "y"), ("x", "core")
    placed = (P(pb, ta), P(pb, ta), P(("row", *ta), pb), P(("row", *ta)))
    return jax.shard_map(
        local, mesh=fine, in_specs=placed, out_specs=P(pb, ("row", *ta)), check_vma=False
    )
```

```python
import jax
import jax.numpy as jnp
from jax import lax
from jax.experimental import pallas as pl
from jax.experimental.pallas import tpu as pltpu
from jax.sharding import Mesh, PartitionSpec as P

NZ, NY, CHUNKS = 8, 4, 2
NT_DIMS = (((1,), (1,)), ((), ()))
RELATIVE = (0, 4, 2, 6, 1, 5, 3, 7)
VMEM_LIMIT = 24 * 1024 * 1024
UP = [(i, (i + 1) % NY) for i in range(NY)]
DOWN = [(i, (i - 1) % NY) for i in range(NY)]


def kernel_matrix(slots, gram, training):
    n, t, depth = training.shape
    rows = gram.shape[1]
    each = t // CHUNKS

    def kernel(slots, gram_ref, training_ref, *refs):
        out_refs, total = refs[:-1], refs[-1]
        step = pl.program_id(0)

        @pl.when(step == 0)
        def _():
            total[...] = jnp.zeros_like(total)

        total[...] += lax.dot_general(training_ref[0], gram_ref[0], NT_DIMS, preferred_element_type=jnp.float32)

        @pl.when(step == n - 1)
        def _():
            for c, out_ref in enumerate(out_refs):
                out_ref[...] = total[c * each : (c + 1) * each].astype(out_ref.dtype)

    return pl.pallas_call(
        kernel,
        out_shape=[jax.ShapeDtypeStruct((each, rows), jnp.bfloat16)] * CHUNKS,
        grid_spec=pltpu.PrefetchScalarGridSpec(
            num_scalar_prefetch=1,
            grid=(n,),
            in_specs=[
                pl.BlockSpec((1, rows, depth), lambda s, slots: (slots[s], 0, 0)),
                pl.BlockSpec((1, t, depth), lambda s, slots: (s, 0, 0)),
            ],
            out_specs=[pl.BlockSpec((each, rows), lambda s, slots: (0, 0))] * CHUNKS,
            scratch_shapes=[pltpu.VMEM((t, rows), jnp.float32)],
        ),
        compiler_params=pltpu.CompilerParams(vmem_limit_bytes=VMEM_LIMIT),
        cost_estimate=pl.CostEstimate(
            flops=2 * n * rows * t * depth, bytes_accessed=2 * n * depth * (rows + t), transcendentals=0
        ),
        name="kernel_matrix",
    )(slots, gram, training)


def score_columns(slots, place, query, blocks, weight, out, chunk):
    n, rows, depth = query.shape
    t = blocks[0][0].shape[1]
    width = NY * t
    columns = weight.shape[1]

    def kernel(slots, place, query_ref, weight_ref, *refs):
        refs = list(refs)
        cut_refs = [[refs.pop(0) for _ in cuts] for cuts in blocks]
        out_ref, ordered, total = refs[-3:]
        step = pl.program_id(0)

        @pl.when(step == 0)
        def _():
            total[...] = jnp.zeros_like(total)

        for d, cuts in enumerate(cut_refs):
            block = cuts[0][0] if len(cuts) == 1 else jnp.where(step < n // 2, cuts[0][0], cuts[1][0])
            ordered[lax.rem(place[0] + d, NY)] = block
        total[...] += lax.dot_general(
            query_ref[0], ordered[...].reshape(width, depth), NT_DIMS, preferred_element_type=jnp.float32
        )

        @pl.when(step == n - 1)
        def _():
            out_ref[...] = total[...] * weight_ref[...]

    operands = [slots, place, query, weight]
    in_specs = [
        pl.BlockSpec((1, rows, depth), lambda s, slots, place: (slots[s], 0, 0)),
        pl.BlockSpec((1, width), lambda s, slots, place: (0, chunk)),
    ]
    for cuts in blocks:
        first = 0
        for cut in cuts:
            size = cut.shape[0]
            in_specs.append(
                pl.BlockSpec(
                    (1, t, depth),
                    lambda s, slots, place, first=first, size=size: (jnp.clip(s - first, 0, size - 1), 0, 0),
                )
            )
            operands.append(cut)
            first += size
    aliases = {}
    if out is not None:
        in_specs.append(pl.BlockSpec(memory_space=pl.ANY))
        aliases = {len(operands): 0}
        operands.append(out)
    return pl.pallas_call(
        kernel,
        out_shape=jax.ShapeDtypeStruct((rows, columns), jnp.float32),
        grid_spec=pltpu.PrefetchScalarGridSpec(
            num_scalar_prefetch=2,
            grid=(n,),
            in_specs=in_specs,
            out_specs=pl.BlockSpec((rows, width), lambda s, slots, place: (0, chunk)),
            scratch_shapes=[pltpu.VMEM((NY, t, depth), jnp.bfloat16), pltpu.VMEM((rows, width), jnp.float32)],
        ),
        input_output_aliases=aliases,
        compiler_params=pltpu.CompilerParams(vmem_limit_bytes=VMEM_LIMIT),
        cost_estimate=pl.CostEstimate(
            flops=2 * n * rows * width * depth, bytes_accessed=2 * n * depth * (rows + width), transcendentals=0
        ),
        name="score_columns",
    )(*operands)


def after(array, *earlier):
    return lax.optimization_barrier((array, earlier))[0]


def exchange(held, distance):
    other = lax.ppermute(held, "z", [(i, i ^ distance) for i in range(NZ)])
    return jnp.concatenate([held, other], axis=0)


def local(query_features, inverse_gram, training_features, residual_weight):
    slots = lax.axis_index("z") ^ jnp.array(RELATIVE, jnp.int32)
    place = lax.axis_index("y").astype(jnp.int32)[None]
    columns, lanes = training_features.shape
    rows, depth = inverse_gram.shape
    t = columns // NY
    each = t // CHUNKS

    folds = depth // lanes
    pieces = training_features.reshape(CHUNKS, NY, each, lanes).transpose(1, 0, 2, 3)
    pieces = pieces.reshape(NY, folds, t // folds, lanes).transpose(0, 2, 1, 3).reshape(NY, t // folds, depth)
    sent = jnp.concatenate([jnp.broadcast_to(inverse_gram, (NY, rows, depth)), pieces], axis=1)
    got = lax.all_to_all(sent, "y", split_axis=0, concat_axis=0, tiled=True)
    gram_rows = got[:, :rows].reshape(NY * rows, depth)
    training = got[:, rows:].reshape(NY, t // folds, folds, lanes).transpose(2, 1, 0, 3).reshape(t, NY * lanes)

    gram = lax.all_gather(gram_rows, ("x", "core"), axis=0)
    query = lax.all_gather(after(query_features, gram_rows), ("x", "core"), axis=0)
    weight = residual_weight[None, :]

    training = exchange(exchange(exchange(training[None], 4), 2), 1)
    a, b = (block[None] for block in kernel_matrix(slots, gram, training))

    half = NZ // 2
    a = exchange(a, 4)
    b = exchange(after(b, a), 4)
    a = exchange(a, 2)
    b = exchange(after(b, a), 2)
    a = exchange(a, 1)
    b = exchange(after(b, a), 1)
    below, above = lax.ppermute(a, "y", UP), lax.ppermute(a, "y", DOWN)
    far = lax.ppermute(below[:half], "y", UP), lax.ppermute(above[half:], "y", DOWN)
    b = after(b, below, above, query)
    below_b, above_b = lax.ppermute(b, "y", UP), lax.ppermute(b, "y", DOWN)
    out = score_columns(slots, place, query, ((a,), (above,), far, (below,)), weight, None, 0)
    first, second = after(below_b[:half], out), after(above_b[half:], out)
    far_b = lax.ppermute(first, "y", UP), lax.ppermute(second, "y", DOWN)
    return score_columns(slots, place, query, ((b,), (above_b,), far_b, (below_b,)), weight, out, 1)


def solution(mesh):
    fine = Mesh(mesh.devices.reshape(NZ, NY, 4, 2, 2), ("z", "y", "x", "core", "row"))
    pb, ta = ("z", "y"), ("x", "core")
    placed = (P(pb, ta), P(pb, ta), P(("row", *ta), pb), P(("row", *ta)))
    return jax.shard_map(
        local, mesh=fine, in_specs=placed, out_specs=P(pb, ("row", *ta)), check_vma=False
    )
```

```python
import jax
import jax.numpy as jnp
from jax import lax
from jax.experimental import pallas as pl
from jax.experimental.pallas import tpu as pltpu
from jax.sharding import Mesh, PartitionSpec as P

NZ, NY, CHUNKS = 8, 4, 2
NT_DIMS = (((1,), (1,)), ((), ()))
RELATIVE = (0, 4, 2, 6, 1, 5, 3, 7)
VMEM_LIMIT = 24 * 1024 * 1024
UP = [(i, (i + 1) % NY) for i in range(NY)]
DOWN = [(i, (i - 1) % NY) for i in range(NY)]


def kernel_matrix(slots, inverse_gram, training):
    n, t, depth = training.shape
    rows = inverse_gram.shape[1]

    def kernel(slots, gram_ref, training_ref, out_ref, total):
        step = pl.program_id(0)

        @pl.when(step == 0)
        def _():
            total[...] = jnp.zeros_like(total)

        total[...] += lax.dot_general(training_ref[0], gram_ref[0], NT_DIMS, preferred_element_type=jnp.float32)

        @pl.when(step == n - 1)
        def _():
            out_ref[...] = total[...].astype(out_ref.dtype)

    return pl.pallas_call(
        kernel,
        out_shape=jax.ShapeDtypeStruct((t, rows), jnp.bfloat16),
        grid_spec=pltpu.PrefetchScalarGridSpec(
            num_scalar_prefetch=1,
            grid=(n,),
            in_specs=[
                pl.BlockSpec((1, rows, depth), lambda s, slots: (slots[s], 0, 0)),
                pl.BlockSpec((1, t, depth), lambda s, slots: (s, 0, 0)),
            ],
            out_specs=pl.BlockSpec((t, rows), lambda s, slots: (0, 0)),
            scratch_shapes=[pltpu.VMEM((t, rows), jnp.float32)],
        ),
        compiler_params=pltpu.CompilerParams(vmem_limit_bytes=VMEM_LIMIT),
        cost_estimate=pl.CostEstimate(
            flops=2 * n * rows * t * depth, bytes_accessed=2 * n * depth * (rows + t), transcendentals=0
        ),
        name="kernel_matrix",
    )(slots, inverse_gram, training)


def score_columns(slots, place, query, chunks, weight, out):
    n, rows, depth = query.shape
    each = chunks[0].shape[1]
    t = each * len(chunks)
    columns = weight.shape[1]

    def kernel(slots, place, query_ref, weight_ref, *refs):
        out_ref, total = refs[-2:]
        step = pl.program_id(0)

        @pl.when(step == 0)
        def _():
            total[...] = jnp.zeros_like(total)

        block = jnp.concatenate([ref[0] for ref in refs[: len(chunks)]], axis=0)
        total[...] += lax.dot_general(query_ref[0], block, NT_DIMS, preferred_element_type=jnp.float32)

        @pl.when(step == n - 1)
        def _():
            out_ref[...] = total[...] * weight_ref[...]

    operands = [slots, place, query, weight, *chunks]
    in_specs = [
        pl.BlockSpec((1, rows, depth), lambda s, slots, place: (slots[s], 0, 0)),
        pl.BlockSpec((1, t), lambda s, slots, place: (0, place[0])),
    ] + [pl.BlockSpec((1, each, depth), lambda s, slots, place: (s, 0, 0))] * len(chunks)
    aliases = {}
    if out is not None:
        in_specs.append(pl.BlockSpec(memory_space=pl.ANY))
        aliases = {len(operands): 0}
        operands.append(out)
    return pl.pallas_call(
        kernel,
        out_shape=jax.ShapeDtypeStruct((rows, columns), jnp.float32),
        grid_spec=pltpu.PrefetchScalarGridSpec(
            num_scalar_prefetch=2,
            grid=(n,),
            in_specs=in_specs,
            out_specs=pl.BlockSpec((rows, t), lambda s, slots, place: (0, place[0])),
            scratch_shapes=[pltpu.VMEM((rows, t), jnp.float32)],
        ),
        input_output_aliases=aliases,
        compiler_params=pltpu.CompilerParams(vmem_limit_bytes=VMEM_LIMIT),
        cost_estimate=pl.CostEstimate(
            flops=2 * n * rows * t * depth, bytes_accessed=2 * n * depth * (rows + t), transcendentals=0
        ),
        name="score_columns",
    )(*operands)


def after(array, *earlier):
    return lax.optimization_barrier((array, earlier))[0]


def exchange(held, distance):
    other = lax.ppermute(held, "z", [(i, i ^ distance) for i in range(NZ)])
    return jnp.concatenate([held, other], axis=0)


def local(query_features, inverse_gram, training_features, residual_weight):
    slots = lax.axis_index("z") ^ jnp.array(RELATIVE, jnp.int32)
    y = lax.axis_index("y").astype(jnp.int32)
    columns, lanes = training_features.shape
    rows, depth = inverse_gram.shape
    t = columns // NY

    folds = depth // lanes
    pieces = training_features.reshape(NY, folds, t // folds, lanes)
    pieces = pieces.transpose(0, 2, 1, 3).reshape(NY, t // folds, depth)
    sent = jnp.concatenate([jnp.broadcast_to(inverse_gram, (NY, rows, depth)), pieces], axis=1)
    got = lax.all_to_all(sent, "y", split_axis=0, concat_axis=0, tiled=True)
    gram_rows = got[:, :rows].reshape(NY * rows, depth)
    training = got[:, rows:].reshape(NY, t // folds, folds, lanes).transpose(2, 1, 0, 3)
    training = training.reshape(CHUNKS, 1, t // CHUNKS, NY * lanes)

    gram = lax.all_gather(gram_rows, ("x", "core"), axis=0)
    query = lax.all_gather(after(query_features, gram_rows), ("x", "core"), axis=0)
    weight = residual_weight[None, :]

    a, b = training[0], training[1]
    for distance in (4, 2, 1):
        a, b = exchange(a, distance), exchange(b, distance)
    a, b = kernel_matrix(slots, gram, a)[None], kernel_matrix(slots, gram, b)[None]
    for distance in (4, 2, 1):
        a, b = exchange(a, distance), exchange(b, distance)

    below_a, above_a = lax.ppermute(a, "y", UP), lax.ppermute(a, "y", DOWN)
    below_b, above_b = lax.ppermute(b, "y", UP), lax.ppermute(b, "y", DOWN)

    def scores(distance, chunks, out):
        return score_columns(slots, lax.rem(y + distance, NY)[None], query, chunks, weight, out)

    out = scores(0, (a, b), None)
    far = lax.ppermute(after(below_a, out), "y", UP), lax.ppermute(after(above_b, out), "y", DOWN)
    out = scores(1, (above_a, above_b), out)
    out = scores(NY - 1, (below_a, below_b), out)
    return scores(2, far, out)


def solution(mesh):
    fine = Mesh(mesh.devices.reshape(NZ, NY, 4, 2, 2), ("z", "y", "x", "core", "row"))
    pb, ta = ("z", "y"), ("x", "core")
    placed = (P(pb, ta), P(pb, ta), P(("row", *ta), pb), P(("row", *ta)))
    return jax.shard_map(
        local, mesh=fine, in_specs=placed, out_specs=P(pb, ("row", *ta)), check_vma=False
    )
```

```python
import jax
import jax.numpy as jnp
from jax import lax
from jax.experimental import pallas as pl
from jax.experimental.pallas import tpu as pltpu
from jax.sharding import Mesh, PartitionSpec as P

NZ, NY, CHUNKS = 8, 4, 2
NT_DIMS = (((1,), (1,)), ((), ()))
RELATIVE = (0, 4, 2, 6, 1, 5, 3, 7)
UP = [(i, (i + 1) % NY) for i in range(NY)]
DOWN = [(i, (i - 1) % NY) for i in range(NY)]


def kernel_matrix(slots, inverse_gram, training):
    n, t, depth = training.shape
    rows = inverse_gram.shape[1]

    def kernel(slots, gram_ref, training_ref, out_ref, total):
        step = pl.program_id(0)

        @pl.when(step == 0)
        def _():
            total[...] = jnp.zeros_like(total)

        total[...] += lax.dot_general(training_ref[0], gram_ref[0], NT_DIMS, preferred_element_type=jnp.float32)

        @pl.when(step == n - 1)
        def _():
            out_ref[...] = total[...].astype(out_ref.dtype)

    return pl.pallas_call(
        kernel,
        out_shape=jax.ShapeDtypeStruct((t, rows), jnp.bfloat16),
        grid_spec=pltpu.PrefetchScalarGridSpec(
            num_scalar_prefetch=1,
            grid=(n,),
            in_specs=[
                pl.BlockSpec((1, rows, depth), lambda s, slots: (slots[s], 0, 0)),
                pl.BlockSpec((1, t, depth), lambda s, slots: (s, 0, 0)),
            ],
            out_specs=pl.BlockSpec((t, rows), lambda s, slots: (0, 0)),
            scratch_shapes=[pltpu.VMEM((t, rows), jnp.float32)],
        ),
        compiler_params=pltpu.CompilerParams(vmem_limit_bytes=51 * 1024 * 1024),
        cost_estimate=pl.CostEstimate(
            flops=2 * n * rows * t * depth, bytes_accessed=2 * n * depth * (rows + t), transcendentals=0
        ),
        name="kernel_matrix",
    )(slots, inverse_gram, training)


def score_columns(slots, place, query, chunks, weight, out):
    n, rows, depth = query.shape
    each = chunks[0].shape[1]
    t = each * len(chunks)
    columns = weight.shape[1]

    def kernel(slots, place, query_ref, weight_ref, *refs):
        out_ref, total = refs[-2:]
        step = pl.program_id(0)

        @pl.when(step == 0)
        def _():
            total[...] = jnp.zeros_like(total)

        block = jnp.concatenate([ref[0] for ref in refs[: len(chunks)]], axis=0)
        total[...] += lax.dot_general(query_ref[0], block, NT_DIMS, preferred_element_type=jnp.float32)

        @pl.when(step == n - 1)
        def _():
            out_ref[...] = total[...] * weight_ref[...]

    operands = [slots, place, query, weight, *chunks]
    in_specs = [
        pl.BlockSpec((1, rows, depth), lambda s, slots, place: (slots[s], 0, 0)),
        pl.BlockSpec((1, t), lambda s, slots, place: (0, place[0])),
    ] + [pl.BlockSpec((1, each, depth), lambda s, slots, place: (s, 0, 0))] * len(chunks)
    aliases = {}
    if out is not None:
        in_specs.append(pl.BlockSpec(memory_space=pl.ANY))
        aliases = {len(operands): 0}
        operands.append(out)
    return pl.pallas_call(
        kernel,
        out_shape=jax.ShapeDtypeStruct((rows, columns), jnp.float32),
        grid_spec=pltpu.PrefetchScalarGridSpec(
            num_scalar_prefetch=2,
            grid=(n,),
            in_specs=in_specs,
            out_specs=pl.BlockSpec((rows, t), lambda s, slots, place: (0, place[0])),
            scratch_shapes=[pltpu.VMEM((rows, t), jnp.float32)],
        ),
        input_output_aliases=aliases,
        compiler_params=pltpu.CompilerParams(vmem_limit_bytes=8 * 1024 * 1024),
        cost_estimate=pl.CostEstimate(
            flops=2 * n * rows * t * depth, bytes_accessed=2 * n * depth * (rows + t), transcendentals=0
        ),
        name="score_columns",
    )(*operands)


def after(array, *earlier):
    return lax.optimization_barrier((array, earlier))[0]


def exchange(held, distance):
    other = lax.ppermute(held, "z", [(i, i ^ distance) for i in range(NZ)])
    return jnp.concatenate([held, other], axis=0)


def local(query_features, inverse_gram, training_features, residual_weight):
    slots = lax.axis_index("z") ^ jnp.array(RELATIVE, jnp.int32)
    y = lax.axis_index("y").astype(jnp.int32)
    columns, lanes = training_features.shape
    rows, depth = inverse_gram.shape
    t = columns // NY

    folds = depth // lanes
    pieces = training_features.reshape(NY, folds, t // folds, lanes)
    pieces = pieces.transpose(0, 2, 1, 3).reshape(NY, t // folds, depth)
    sent = jnp.concatenate([jnp.broadcast_to(inverse_gram, (NY, rows, depth)), pieces], axis=1)
    got = lax.all_to_all(sent, "y", split_axis=0, concat_axis=0, tiled=True)
    gram_rows = got[:, :rows].reshape(NY * rows, depth)
    training = got[:, rows:].reshape(NY, t // folds, folds, lanes).transpose(2, 1, 0, 3)
    training = training.reshape(CHUNKS, 1, t // CHUNKS, NY * lanes)

    gram = lax.all_gather(gram_rows, ("x", "core"), axis=0)
    query = lax.all_gather(after(query_features, gram_rows), ("x", "core"), axis=0)
    weight = residual_weight[None, :]

    a, b = training[0], training[1]
    for distance in (4, 2, 1):
        a, b = exchange(a, distance), exchange(b, distance)
    a, b = kernel_matrix(slots, gram, a)[None], kernel_matrix(slots, gram, b)[None]
    for distance in (4, 2, 1):
        a, b = exchange(a, distance), exchange(b, distance)

    below_a, above_a = lax.ppermute(a, "y", UP), lax.ppermute(a, "y", DOWN)
    below_b, above_b = lax.ppermute(b, "y", UP), lax.ppermute(b, "y", DOWN)

    def scores(distance, chunks, out):
        return score_columns(slots, lax.rem(y + distance, NY)[None], query, chunks, weight, out)

    out = scores(0, (a, b), None)
    far = lax.ppermute(after(below_a, out), "y", UP), lax.ppermute(after(above_b, out), "y", DOWN)
    out = scores(1, (above_a, above_b), out)
    out = scores(NY - 1, (below_a, below_b), out)
    return scores(2, far, out)


def solution(mesh):
    fine = Mesh(mesh.devices.reshape(NZ, NY, 4, 2, 2), ("z", "y", "x", "core", "row"))
    pb, ta = ("z", "y"), ("x", "core")
    placed = (P(pb, ta), P(pb, ta), P(("row", *ta), pb), P(("row", *ta)))
    return jax.shard_map(
        local, mesh=fine, in_specs=placed, out_specs=P(pb, ("row", *ta)), check_vma=False
    )
```

```python
import jax
import jax.numpy as jnp
from jax import lax
from jax.experimental import pallas as pl
from jax.experimental.pallas import tpu as pltpu
from jax.sharding import Mesh, PartitionSpec as P

NZ, NY, CHUNKS = 8, 4, 2
NT_DIMS = (((1,), (1,)), ((), ()))
RELATIVE = (0, 4, 2, 6, 1, 5, 3, 7)
VMEM_LIMIT = 24 * 1024 * 1024
UP = [(i, (i + 1) % NY) for i in range(NY)]
DOWN = [(i, (i - 1) % NY) for i in range(NY)]


def kernel_matrix(slots, inverse_gram, training):
    n, t, depth = training.shape
    rows = inverse_gram.shape[1]

    def kernel(slots, gram_ref, training_ref, out_ref, total):
        step = pl.program_id(0)

        @pl.when(step == 0)
        def _():
            total[...] = jnp.zeros_like(total)

        total[...] += lax.dot_general(training_ref[0], gram_ref[0], NT_DIMS, preferred_element_type=jnp.float32)

        @pl.when(step == n - 1)
        def _():
            out_ref[...] = total[...].astype(out_ref.dtype)

    return pl.pallas_call(
        kernel,
        out_shape=jax.ShapeDtypeStruct((t, rows), jnp.bfloat16),
        grid_spec=pltpu.PrefetchScalarGridSpec(
            num_scalar_prefetch=1,
            grid=(n,),
            in_specs=[
                pl.BlockSpec((1, rows, depth), lambda s, slots: (slots[s], 0, 0)),
                pl.BlockSpec((1, t, depth), lambda s, slots: (s, 0, 0)),
            ],
            out_specs=pl.BlockSpec((t, rows), lambda s, slots: (0, 0)),
            scratch_shapes=[pltpu.VMEM((t, rows), jnp.float32)],
        ),
        compiler_params=pltpu.CompilerParams(vmem_limit_bytes=VMEM_LIMIT),
        cost_estimate=pl.CostEstimate(
            flops=2 * n * rows * t * depth, bytes_accessed=2 * n * depth * (rows + t), transcendentals=0
        ),
        name="kernel_matrix",
    )(slots, inverse_gram, training)


def score_columns(slots, place, query, chunks, weight, out):
    n, rows, depth = query.shape
    each = chunks[0].shape[1]
    t = each * len(chunks)
    columns = weight.shape[1]

    def kernel(slots, place, query_ref, weight_ref, *refs):
        out_ref, total = refs[-2:]
        step = pl.program_id(0)

        @pl.when(step == 0)
        def _():
            total[...] = jnp.zeros_like(total)

        block = jnp.concatenate([ref[step] for ref in refs[: len(chunks)]], axis=0)
        total[...] += lax.dot_general(query_ref[0], block, NT_DIMS, preferred_element_type=jnp.float32)

        @pl.when(step == n - 1)
        def _():
            out_ref[...] = total[...] * weight_ref[...]

    operands = [slots, place, query, weight, *chunks]
    in_specs = [
        pl.BlockSpec((1, rows, depth), lambda s, slots, place: (slots[s], 0, 0)),
        pl.BlockSpec((1, t), lambda s, slots, place: (0, place[0])),
    ] + [pl.BlockSpec((n, each, depth), lambda s, slots, place: (0, 0, 0))] * len(chunks)
    aliases = {}
    if out is not None:
        in_specs.append(pl.BlockSpec(memory_space=pl.ANY))
        aliases = {len(operands): 0}
        operands.append(out)
    return pl.pallas_call(
        kernel,
        out_shape=jax.ShapeDtypeStruct((rows, columns), jnp.float32),
        grid_spec=pltpu.PrefetchScalarGridSpec(
            num_scalar_prefetch=2,
            grid=(n,),
            in_specs=in_specs,
            out_specs=pl.BlockSpec((rows, t), lambda s, slots, place: (0, place[0])),
            scratch_shapes=[pltpu.VMEM((rows, t), jnp.float32)],
        ),
        input_output_aliases=aliases,
        compiler_params=pltpu.CompilerParams(vmem_limit_bytes=VMEM_LIMIT),
        cost_estimate=pl.CostEstimate(
            flops=2 * n * rows * t * depth, bytes_accessed=2 * n * depth * (rows + t), transcendentals=0
        ),
        name="score_columns",
    )(*operands)


def after(array, *earlier):
    return lax.optimization_barrier((array, earlier))[0]


def exchange(held, distance):
    other = lax.ppermute(held, "z", [(i, i ^ distance) for i in range(NZ)])
    return jnp.concatenate([held, other], axis=0)


def local(query_features, inverse_gram, training_features, residual_weight):
    slots = lax.axis_index("z") ^ jnp.array(RELATIVE, jnp.int32)
    y = lax.axis_index("y").astype(jnp.int32)
    columns, lanes = training_features.shape
    rows, depth = inverse_gram.shape
    t = columns // NY

    folds = depth // lanes
    pieces = training_features.reshape(NY, folds, t // folds, lanes)
    pieces = pieces.transpose(0, 2, 1, 3).reshape(NY, t // folds, depth)
    sent = jnp.concatenate([jnp.broadcast_to(inverse_gram, (NY, rows, depth)), pieces], axis=1)
    got = lax.all_to_all(sent, "y", split_axis=0, concat_axis=0, tiled=True)
    gram_rows = got[:, :rows].reshape(NY * rows, depth)
    training = got[:, rows:].reshape(NY, t // folds, folds, lanes).transpose(2, 1, 0, 3)
    training = training.reshape(CHUNKS, 1, t // CHUNKS, NY * lanes)

    gram = lax.all_gather(gram_rows, ("x", "core"), axis=0)
    query = lax.all_gather(after(query_features, gram_rows), ("x", "core"), axis=0)
    weight = residual_weight[None, :]

    a, b = training[0], training[1]
    for distance in (4, 2, 1):
        a, b = exchange(a, distance), exchange(b, distance)
    a, b = kernel_matrix(slots, gram, a)[None], kernel_matrix(slots, gram, b)[None]
    for distance in (4, 2, 1):
        a, b = exchange(a, distance), exchange(b, distance)

    below_a, above_a = lax.ppermute(a, "y", UP), lax.ppermute(a, "y", DOWN)
    below_b, above_b = lax.ppermute(b, "y", UP), lax.ppermute(b, "y", DOWN)

    def scores(distance, chunks, out):
        return score_columns(slots, lax.rem(y + distance, NY)[None], query, chunks, weight, out)

    out = scores(0, (a, b), None)
    far = lax.ppermute(below_a, "y", UP), lax.ppermute(above_b, "y", DOWN)
    out = scores(1, (above_a, above_b), out)
    out = scores(NY - 1, (below_a, below_b), out)
    return scores(2, far, out)


def solution(mesh):
    fine = Mesh(mesh.devices.reshape(NZ, NY, 4, 2, 2), ("z", "y", "x", "core", "row"))
    pb, ta = ("z", "y"), ("x", "core")
    placed = (P(pb, ta), P(pb, ta), P(("row", *ta), pb), P(("row", *ta)))
    return jax.shard_map(
        local, mesh=fine, in_specs=placed, out_specs=P(pb, ("row", *ta)), check_vma=False
    )
```

```python
import jax
import jax.numpy as jnp
from jax import lax
from jax.experimental import pallas as pl
from jax.experimental.pallas import tpu as pltpu
from jax.sharding import Mesh, PartitionSpec as P

NZ, NY, CHUNKS = 8, 4, 2
NT_DIMS = (((1,), (1,)), ((), ()))
RELATIVE = (0, 4, 2, 6, 1, 5, 3, 7)
VMEM_LIMIT = 24 * 1024 * 1024
UP = [(i, (i + 1) % NY) for i in range(NY)]
DOWN = [(i, (i - 1) % NY) for i in range(NY)]


def kernel_matrix(slots, inverse_gram, training):
    n, t, depth = training.shape
    rows = inverse_gram.shape[1]

    def kernel(slots, gram_ref, training_ref, out_ref, total):
        step = pl.program_id(0)

        @pl.when(step == 0)
        def _():
            total[...] = jnp.zeros_like(total)

        total[...] += lax.dot_general(training_ref[0], gram_ref[0], NT_DIMS, preferred_element_type=jnp.float32)

        @pl.when(step == n - 1)
        def _():
            out_ref[...] = total[...].astype(out_ref.dtype)

    return pl.pallas_call(
        kernel,
        out_shape=jax.ShapeDtypeStruct((t, rows), jnp.bfloat16),
        grid_spec=pltpu.PrefetchScalarGridSpec(
            num_scalar_prefetch=1,
            grid=(n,),
            in_specs=[
                pl.BlockSpec((1, rows, depth), lambda s, slots: (slots[s], 0, 0)),
                pl.BlockSpec((1, t, depth), lambda s, slots: (s, 0, 0)),
            ],
            out_specs=pl.BlockSpec((t, rows), lambda s, slots: (0, 0)),
            scratch_shapes=[pltpu.VMEM((t, rows), jnp.float32)],
        ),
        compiler_params=pltpu.CompilerParams(vmem_limit_bytes=VMEM_LIMIT),
        cost_estimate=pl.CostEstimate(
            flops=2 * n * rows * t * depth, bytes_accessed=2 * n * depth * (rows + t), transcendentals=0
        ),
        name="kernel_matrix",
    )(slots, inverse_gram, training)


def score_columns(slots, place, query, first, second, weight, out):
    n, rows, depth = query.shape
    each = first.shape[1]
    t = each * CHUNKS
    columns = weight.shape[1]
    half = n // 2

    def kernel(slots, place, query_ref, weight_ref, first_ref, near_ref, other_ref, *refs):
        out_ref, total = refs[-2:]
        step = pl.program_id(0)

        @pl.when(step == 0)
        def _():
            total[...] = jnp.zeros_like(total)

        near, other = near_ref[0, jnp.minimum(step, half - 1)], other_ref[0, jnp.maximum(step - half, 0)]
        block = jnp.concatenate([first_ref[step], jnp.where(step < half, near, other)], axis=0)
        total[...] += lax.dot_general(query_ref[0], block, NT_DIMS, preferred_element_type=jnp.float32)

        @pl.when(step == n - 1)
        def _():
            out_ref[...] = total[...] * weight_ref[...]

    operands = [slots, place, query, weight, first] + [array for array, _ in second]
    in_specs = [
        pl.BlockSpec((1, rows, depth), lambda s, slots, place: (slots[s], 0, 0)),
        pl.BlockSpec((1, t), lambda s, slots, place: (0, place[0])),
        pl.BlockSpec((n, each, depth), lambda s, slots, place: (0, 0, 0)),
    ] + [
        pl.BlockSpec((1, half, each, depth), lambda s, slots, place, index=index: (index, 0, 0, 0)) for _, index in second
    ]
    aliases = {}
    if out is not None:
        in_specs.append(pl.BlockSpec(memory_space=pl.ANY))
        aliases = {len(operands): 0}
        operands.append(out)
    return pl.pallas_call(
        kernel,
        out_shape=jax.ShapeDtypeStruct((rows, columns), jnp.float32),
        grid_spec=pltpu.PrefetchScalarGridSpec(
            num_scalar_prefetch=2,
            grid=(n,),
            in_specs=in_specs,
            out_specs=pl.BlockSpec((rows, t), lambda s, slots, place: (0, place[0])),
            scratch_shapes=[pltpu.VMEM((rows, t), jnp.float32)],
        ),
        input_output_aliases=aliases,
        compiler_params=pltpu.CompilerParams(vmem_limit_bytes=VMEM_LIMIT),
        cost_estimate=pl.CostEstimate(
            flops=2 * n * rows * t * depth, bytes_accessed=2 * n * depth * (rows + t), transcendentals=0
        ),
        name="score_columns",
    )(*operands)


def after(array, *earlier):
    return lax.optimization_barrier((array, earlier))[0]


def swapped(held, distance):
    return lax.ppermute(held, "z", [(i, i ^ distance) for i in range(NZ)])


def exchange(held, distance):
    return jnp.concatenate([held, swapped(held, distance)], axis=0)


def local(query_features, inverse_gram, training_features, residual_weight):
    slots = lax.axis_index("z") ^ jnp.array(RELATIVE, jnp.int32)
    y = lax.axis_index("y").astype(jnp.int32)
    columns, lanes = training_features.shape
    rows, depth = inverse_gram.shape
    t = columns // NY

    folds = depth // lanes
    pieces = training_features.reshape(NY, folds, t // folds, lanes)
    pieces = pieces.transpose(0, 2, 1, 3).reshape(NY, t // folds, depth)
    sent = jnp.concatenate([jnp.broadcast_to(inverse_gram, (NY, rows, depth)), pieces], axis=1)
    got = lax.all_to_all(sent, "y", split_axis=0, concat_axis=0, tiled=True)
    gram_rows = got[:, :rows].reshape(NY * rows, depth)
    training = got[:, rows:].reshape(NY, t // folds, folds, lanes).transpose(2, 1, 0, 3)
    training = training.reshape(CHUNKS, 1, t // CHUNKS, NY * lanes)

    gram = lax.all_gather(gram_rows, ("x", "core"), axis=0)
    query = lax.all_gather(after(query_features, gram_rows), ("x", "core"), axis=0)
    weight = residual_weight[None, :]

    a, b = training[0], training[1]
    for distance in (4, 2, 1):
        a, b = exchange(after(a, b), distance), exchange(b, distance)
    b = kernel_matrix(slots, gram, b)[None]
    a = kernel_matrix(slots, gram, after(a, b))[None]
    for distance in (4, 2):
        a, b = exchange(after(a, b), distance), exchange(b, distance)

    b = b[None]
    a = exchange(after(a, b), 1)
    below_b, above_b = lax.ppermute(b, "y", UP), lax.ppermute(b, "y", DOWN)
    far_b = lax.ppermute(above_b, "y", DOWN)
    a = after(a, below_b, above_b)
    below_a, above_a = lax.ppermute(a, "y", UP), lax.ppermute(a, "y", DOWN)
    far_a = lax.ppermute(below_a, "y", UP)
    own = swapped(b, 1)
    near = swapped(after(jnp.concatenate([below_b, above_b], axis=0), own), 1)

    def scores(distance, first, second, out):
        return score_columns(slots, lax.rem(y + distance, NY)[None], query, first, second, weight, out)

    out = scores(0, a, ((b, 0), (own, 0)), None)
    out = scores(1, above_a, ((above_b, 0), (near, 1)), out)
    out = scores(NY - 1, below_a, ((below_b, 0), (near, 0)), out)
    return scores(2, far_a, ((far_b, 0), (swapped(far_b, 1), 0)), out)


def solution(mesh):
    fine = Mesh(mesh.devices.reshape(NZ, NY, 4, 2, 2), ("z", "y", "x", "core", "row"))
    pb, ta = ("z", "y"), ("x", "core")
    placed = (P(pb, ta), P(pb, ta), P(("row", *ta), pb), P(("row", *ta)))
    return jax.shard_map(
        local, mesh=fine, in_specs=placed, out_specs=P(pb, ("row", *ta)), check_vma=False
    )
```

```python
import jax
import jax.numpy as jnp
from jax import lax
from jax.experimental import pallas as pl
from jax.experimental.pallas import tpu as pltpu
from jax.sharding import Mesh, PartitionSpec as P

NZ, NY, CHUNKS = 8, 4, 2
NT_DIMS = (((1,), (1,)), ((), ()))
RELATIVE = (0, 4, 2, 6, 1, 5, 3, 7)
VMEM_LIMIT = 24 * 1024 * 1024
UP = [(i, (i + 1) % NY) for i in range(NY)]
DOWN = [(i, (i - 1) % NY) for i in range(NY)]


def kernel_matrix(slots, gram, chunks):
    n, t, depth = chunks[0].shape
    rows = gram.shape[1]
    count = len(chunks)

    def kernel(slots, gram_ref, *refs):
        chunk_refs, out_refs, total = refs[:count], refs[count:-1], refs[-1]
        step = pl.program_id(0)

        @pl.when(step == 0)
        def _():
            total[...] = jnp.zeros_like(total)

        both = jnp.concatenate([ref[0] for ref in chunk_refs], axis=0)
        total[...] += lax.dot_general(both, gram_ref[0], NT_DIMS, preferred_element_type=jnp.float32)

        @pl.when(step == n - 1)
        def _():
            for c, out_ref in enumerate(out_refs):
                out_ref[...] = total[c * t : (c + 1) * t].astype(out_ref.dtype)

    return pl.pallas_call(
        kernel,
        out_shape=[jax.ShapeDtypeStruct((t, rows), jnp.bfloat16)] * count,
        grid_spec=pltpu.PrefetchScalarGridSpec(
            num_scalar_prefetch=1,
            grid=(n,),
            in_specs=[pl.BlockSpec((1, rows, depth), lambda s, slots: (slots[s], 0, 0))]
            + [pl.BlockSpec((1, t, depth), lambda s, slots: (s, 0, 0))] * count,
            out_specs=[pl.BlockSpec((t, rows), lambda s, slots: (0, 0))] * count,
            scratch_shapes=[pltpu.VMEM((count * t, rows), jnp.float32)],
        ),
        compiler_params=pltpu.CompilerParams(vmem_limit_bytes=VMEM_LIMIT),
        cost_estimate=pl.CostEstimate(
            flops=2 * n * rows * count * t * depth,
            bytes_accessed=2 * n * depth * (rows + count * t),
            transcendentals=0,
        ),
        name="kernel_matrix",
    )(slots, gram, *chunks)


def score_columns(slots, place, query, chunks, weight, out):
    n, rows, depth = query.shape
    each = chunks[0].shape[1]
    t = each * len(chunks)
    columns = weight.shape[1]

    def kernel(slots, place, query_ref, weight_ref, *refs):
        out_ref, total = refs[-2:]
        step = pl.program_id(0)

        @pl.when(step == 0)
        def _():
            total[...] = jnp.zeros_like(total)

        block = jnp.concatenate([ref[step] for ref in refs[: len(chunks)]], axis=0)
        total[...] += lax.dot_general(query_ref[0], block, NT_DIMS, preferred_element_type=jnp.float32)

        @pl.when(step == n - 1)
        def _():
            out_ref[...] = total[...] * weight_ref[...]

    operands = [slots, place, query, weight, *chunks]
    in_specs = [
        pl.BlockSpec((1, rows, depth), lambda s, slots, place: (slots[s], 0, 0)),
        pl.BlockSpec((1, t), lambda s, slots, place: (0, place[0])),
    ] + [pl.BlockSpec((n, each, depth), lambda s, slots, place: (0, 0, 0))] * len(chunks)
    aliases = {}
    if out is not None:
        in_specs.append(pl.BlockSpec(memory_space=pl.ANY))
        aliases = {len(operands): 0}
        operands.append(out)
    return pl.pallas_call(
        kernel,
        out_shape=jax.ShapeDtypeStruct((rows, columns), jnp.float32),
        grid_spec=pltpu.PrefetchScalarGridSpec(
            num_scalar_prefetch=2,
            grid=(n,),
            in_specs=in_specs,
            out_specs=pl.BlockSpec((rows, t), lambda s, slots, place: (0, place[0])),
            scratch_shapes=[pltpu.VMEM((rows, t), jnp.float32)],
        ),
        input_output_aliases=aliases,
        compiler_params=pltpu.CompilerParams(vmem_limit_bytes=VMEM_LIMIT),
        cost_estimate=pl.CostEstimate(
            flops=2 * n * rows * t * depth, bytes_accessed=2 * n * depth * (rows + t), transcendentals=0
        ),
        name="score_columns",
    )(*operands)


def after(array, *earlier):
    return lax.optimization_barrier((array, earlier))[0]


def exchange(held, distance):
    other = lax.ppermute(held, "z", [(i, i ^ distance) for i in range(NZ)])
    return jnp.concatenate([held, other], axis=0)


def local(query_features, inverse_gram, training_features, residual_weight):
    slots = lax.axis_index("z") ^ jnp.array(RELATIVE, jnp.int32)
    y = lax.axis_index("y").astype(jnp.int32)
    columns, lanes = training_features.shape
    rows, depth = inverse_gram.shape
    t = columns // NY

    folds = depth // lanes
    pieces = training_features.reshape(NY, folds, t // folds, lanes)
    pieces = pieces.transpose(0, 2, 1, 3).reshape(NY, t // folds, depth)
    sent = jnp.concatenate([jnp.broadcast_to(inverse_gram, (NY, rows, depth)), pieces], axis=1)
    got = lax.all_to_all(sent, "y", split_axis=0, concat_axis=0, tiled=True)
    gram_rows = got[:, :rows].reshape(NY * rows, depth)
    training = got[:, rows:].reshape(NY, t // folds, folds, lanes).transpose(2, 1, 0, 3)
    training = training.reshape(CHUNKS, 1, t // CHUNKS, NY * lanes)

    gram = lax.all_gather(gram_rows, ("x", "core"), axis=0)
    query = lax.all_gather(after(query_features, gram_rows), ("x", "core"), axis=0)
    weight = residual_weight[None, :]

    a, b = training[0], training[1]
    for distance in (4, 2, 1):
        a, b = exchange(a, distance), exchange(b, distance)
    a, b = (block[None] for block in kernel_matrix(slots, gram, (a, b)))
    for distance in (4, 2, 1):
        a, b = exchange(a, distance), exchange(b, distance)

    below_a, above_a = lax.ppermute(a, "y", UP), lax.ppermute(a, "y", DOWN)
    below_b, above_b = lax.ppermute(b, "y", UP), lax.ppermute(b, "y", DOWN)

    def scores(distance, chunks, out):
        return score_columns(slots, lax.rem(y + distance, NY)[None], query, chunks, weight, out)

    out = scores(0, (a, b), None)
    far = lax.ppermute(below_a, "y", UP), lax.ppermute(above_b, "y", DOWN)
    out = scores(1, (above_a, above_b), out)
    out = scores(NY - 1, (below_a, below_b), out)
    return scores(2, far, out)


def solution(mesh):
    fine = Mesh(mesh.devices.reshape(NZ, NY, 4, 2, 2), ("z", "y", "x", "core", "row"))
    pb, ta = ("z", "y"), ("x", "core")
    placed = (P(pb, ta), P(pb, ta), P(("row", *ta), pb), P(("row", *ta)))
    return jax.shard_map(
        local, mesh=fine, in_specs=placed, out_specs=P(pb, ("row", *ta)), check_vma=False
    )
```

```python
import jax
import jax.numpy as jnp
from jax import lax
from jax.experimental import pallas as pl
from jax.experimental.pallas import tpu as pltpu
from jax.sharding import Mesh, PartitionSpec as P

NZ, NY = 8, 4
NT_DIMS = (((1,), (1,)), ((), ()))
RELATIVE = (1, 5, 3, 7, 0, 4, 2, 6)
VMEM_LIMIT = 24 * 1024 * 1024
UP = [(i, (i + 1) % NY) for i in range(NY)]
DOWN = [(i, (i - 1) % NY) for i in range(NY)]


def kernel_matrix(slots, gram, training):
    n, t, depth = training.shape
    rows = gram.shape[1]

    def kernel(slots, gram_ref, training_ref, out_ref, total):
        step = pl.program_id(0)

        @pl.when(step == 0)
        def _():
            total[...] = jnp.zeros_like(total)

        total[...] += lax.dot_general(training_ref[0], gram_ref[0], NT_DIMS, preferred_element_type=jnp.float32)

        @pl.when(step == n - 1)
        def _():
            out_ref[...] = total[...].astype(out_ref.dtype)

    return pl.pallas_call(
        kernel,
        out_shape=jax.ShapeDtypeStruct((t, rows), jnp.bfloat16),
        grid_spec=pltpu.PrefetchScalarGridSpec(
            num_scalar_prefetch=1,
            grid=(n,),
            in_specs=[
                pl.BlockSpec((1, rows, depth), lambda s, slots: (slots[s], 0, 0)),
                pl.BlockSpec((1, t, depth), lambda s, slots: (s, 0, 0)),
            ],
            out_specs=pl.BlockSpec((t, rows), lambda s, slots: (0, 0)),
            scratch_shapes=[pltpu.VMEM((t, rows), jnp.float32)],
        ),
        compiler_params=pltpu.CompilerParams(vmem_limit_bytes=VMEM_LIMIT),
        cost_estimate=pl.CostEstimate(
            flops=2 * n * rows * t * depth, bytes_accessed=2 * n * depth * (rows + t), transcendentals=0
        ),
        name="kernel_matrix",
    )(slots, gram, training)


def score_columns(slots, place, query, halves, weight, out):
    n, rows, depth = query.shape
    half, t, _ = halves[0].shape
    columns = weight.shape[1]

    def kernel(slots, place, query_ref, weight_ref, first_ref, second_ref, *refs):
        out_ref, total = refs[-2:]
        step = pl.program_id(0)

        @pl.when(step == 0)
        def _():
            total[...] = jnp.zeros_like(total)

        first, second = first_ref[jnp.minimum(step, half - 1)], second_ref[jnp.maximum(step - half, 0)]
        block = jnp.where(step < half, first, second)
        total[...] += lax.dot_general(query_ref[0], block, NT_DIMS, preferred_element_type=jnp.float32)

        @pl.when(step == n - 1)
        def _():
            out_ref[...] = total[...] * weight_ref[...]

    operands = [slots, place, query, weight, *halves]
    in_specs = [
        pl.BlockSpec((1, rows, depth), lambda s, slots, place: (slots[s], 0, 0)),
        pl.BlockSpec((1, t), lambda s, slots, place: (0, place[0])),
    ] + [pl.BlockSpec((half, t, depth), lambda s, slots, place: (0, 0, 0))] * 2
    aliases = {}
    if out is not None:
        in_specs.append(pl.BlockSpec(memory_space=pl.ANY))
        aliases = {len(operands): 0}
        operands.append(out)
    return pl.pallas_call(
        kernel,
        out_shape=jax.ShapeDtypeStruct((rows, columns), jnp.float32),
        grid_spec=pltpu.PrefetchScalarGridSpec(
            num_scalar_prefetch=2,
            grid=(n,),
            in_specs=in_specs,
            out_specs=pl.BlockSpec((rows, t), lambda s, slots, place: (0, place[0])),
            scratch_shapes=[pltpu.VMEM((rows, t), jnp.float32)],
        ),
        input_output_aliases=aliases,
        compiler_params=pltpu.CompilerParams(vmem_limit_bytes=VMEM_LIMIT),
        cost_estimate=pl.CostEstimate(
            flops=2 * n * rows * t * depth, bytes_accessed=2 * n * depth * (rows + t), transcendentals=0
        ),
        name="score_columns",
    )(*operands)


def swapped(held, distance):
    return lax.ppermute(held, "z", [(i, i ^ distance) for i in range(NZ)])


def gather_z(block):
    pair = jnp.stack([block, swapped(block, 4)])
    first = jnp.concatenate([swapped(pair, 1), swapped(pair, 3)], axis=0)
    second = jnp.concatenate([pair, swapped(pair, 2)], axis=0)
    return first, second


def local(query_features, inverse_gram, training_features, residual_weight):
    slots = lax.axis_index("z") ^ jnp.array(RELATIVE, jnp.int32)
    y = lax.axis_index("y").astype(jnp.int32)
    columns, lanes = training_features.shape
    rows, depth = inverse_gram.shape
    t = columns // NY

    folds = depth // lanes
    pieces = training_features.reshape(NY, folds, t // folds, lanes)
    pieces = pieces.transpose(0, 2, 1, 3).reshape(NY, t // folds, depth)
    sent = jnp.concatenate([jnp.broadcast_to(inverse_gram, (NY, rows, depth)), pieces], axis=1)
    got = lax.all_to_all(sent, "y", split_axis=0, concat_axis=0, tiled=True)
    gram_rows = got[:, :rows].reshape(NY * rows, depth)
    training = got[:, rows:].reshape(NY, t // folds, folds, lanes).transpose(2, 1, 0, 3)
    training = training.reshape(t, NY * lanes)

    gram = lax.all_gather(gram_rows, ("x", "core"), axis=0)
    query = lax.all_gather(query_features, ("x", "core"), axis=0)
    weight = residual_weight[None, :]

    training = jnp.concatenate(gather_z(training), axis=0)
    a, b = gather_z(kernel_matrix(slots, gram, training))

    below_a, above_a = lax.ppermute(a, "y", UP), lax.ppermute(a, "y", DOWN)
    below_b, above_b = lax.ppermute(b, "y", UP), lax.ppermute(b, "y", DOWN)

    def scores(distance, halves, out):
        return score_columns(slots, lax.rem(y + distance, NY)[None], query, halves, weight, out)

    out = scores(0, (a, b), None)
    far = lax.ppermute(below_a, "y", UP), lax.ppermute(above_b, "y", DOWN)
    out = scores(1, (above_a, above_b), out)
    out = scores(NY - 1, (below_a, below_b), out)
    return scores(2, far, out)


def solution(mesh):
    fine = Mesh(mesh.devices.reshape(NZ, NY, 4, 2, 2), ("z", "y", "x", "core", "row"))
    pb, ta = ("z", "y"), ("x", "core")
    placed = (P(pb, ta), P(pb, ta), P(("row", *ta), pb), P(("row", *ta)))
    return jax.shard_map(
        local, mesh=fine, in_specs=placed, out_specs=P(pb, ("row", *ta)), check_vma=False
    )
```

```python
import jax
import jax.numpy as jnp
from jax import lax
from jax.experimental import pallas as pl
from jax.experimental.pallas import tpu as pltpu
from jax.sharding import Mesh, PartitionSpec as P

NZ, NY, CHUNKS = 8, 4, 2
NT_DIMS = (((1,), (1,)), ((), ()))
RELATIVE = (0, 4, 2, 6, 1, 5, 3, 7)
VMEM_LIMIT = 16 * 1024 * 1024
UP = [(i, (i + 1) % NY) for i in range(NY)]
DOWN = [(i, (i - 1) % NY) for i in range(NY)]


def pack(inverse_gram, training_features):
    rows, depth = inverse_gram.shape
    columns, lanes = training_features.shape
    t, folds = columns // NY, depth // lanes
    each = t // folds

    def kernel(gram_ref, training_ref, out_ref):
        for k in range(NY):
            out_ref[k, :rows] = gram_ref[...]
            for f in range(folds):
                first = k * t + f * each
                out_ref[k, rows:, f * lanes : (f + 1) * lanes] = training_ref[first : first + each]

    return pl.pallas_call(
        kernel,
        out_shape=jax.ShapeDtypeStruct((NY, rows + each, depth), jnp.bfloat16),
        in_specs=[pl.BlockSpec(memory_space=pltpu.VMEM)] * 2,
        out_specs=pl.BlockSpec(memory_space=pltpu.VMEM),
        compiler_params=pltpu.CompilerParams(vmem_limit_bytes=VMEM_LIMIT),
        name="pack",
    )(inverse_gram, training_features)


def kernel_matrix(slots, gram, training):
    n, t, depth = training.shape
    rows = gram.shape[1]

    def kernel(slots, gram_ref, training_ref, out_ref):
        total = jnp.zeros((t, rows), jnp.float32)
        for s in range(n):
            total += lax.dot_general(training_ref[s], gram_ref[slots[s]], NT_DIMS, preferred_element_type=jnp.float32)
        out_ref[...] = total.astype(out_ref.dtype)

    return pl.pallas_call(
        kernel,
        out_shape=jax.ShapeDtypeStruct((t, rows), jnp.bfloat16),
        in_specs=[pl.BlockSpec(memory_space=pltpu.SMEM)] + [pl.BlockSpec(memory_space=pltpu.VMEM)] * 2,
        out_specs=pl.BlockSpec(memory_space=pltpu.VMEM),
        compiler_params=pltpu.CompilerParams(vmem_limit_bytes=VMEM_LIMIT),
        cost_estimate=pl.CostEstimate(
            flops=2 * n * rows * t * depth, bytes_accessed=2 * n * depth * (rows + t), transcendentals=0
        ),
        name="kernel_matrix",
    )(slots, gram, training)


def score_columns(slots, place, query, chunks, weight, out):
    n, rows, depth = query.shape
    t = sum(chunk.shape[1] for chunk in chunks)
    columns = weight.shape[1]

    def kernel(slots, place, query_ref, weight_ref, *refs):
        chunk_refs = refs[: len(chunks)]
        out_ref, total, sent = refs[-3:]
        span = pl.ds(pl.multiple_of(place[0] * t, t), t)
        for s in range(n):
            block = jnp.concatenate([ref[s] for ref in chunk_refs], axis=0)
            product = lax.dot_general(query_ref[slots[s]], block, NT_DIMS, preferred_element_type=jnp.float32)
            if s == 0:
                total[...] = product
            elif s < n - 1:
                total[...] += product
            else:
                total[...] = (total[...] + product) * weight_ref[:, span]
        copy = pltpu.make_async_copy(total, out_ref.at[:, span], sent)
        copy.start()
        copy.wait()

    operands = [slots, place, query, weight, *chunks]
    in_specs = [pl.BlockSpec(memory_space=pltpu.SMEM)] * 2 + [pl.BlockSpec(memory_space=pltpu.VMEM)] * (2 + len(chunks))
    aliases = {}
    if out is not None:
        in_specs.append(pl.BlockSpec(memory_space=pl.ANY))
        aliases = {len(operands): 0}
        operands.append(out)
    return pl.pallas_call(
        kernel,
        out_shape=jax.ShapeDtypeStruct((rows, columns), jnp.float32),
        in_specs=in_specs,
        out_specs=pl.BlockSpec(memory_space=pl.ANY),
        scratch_shapes=[pltpu.VMEM((rows, t), jnp.float32), pltpu.SemaphoreType.DMA],
        input_output_aliases=aliases,
        compiler_params=pltpu.CompilerParams(vmem_limit_bytes=VMEM_LIMIT),
        cost_estimate=pl.CostEstimate(
            flops=2 * n * rows * t * depth, bytes_accessed=2 * n * depth * (rows + t), transcendentals=0
        ),
        name="score_columns",
    )(*operands)


def after(array, *earlier):
    return lax.optimization_barrier((array, earlier))[0]


def exchange(held, distance):
    other = lax.ppermute(held, "z", [(i, i ^ distance) for i in range(NZ)])
    return jnp.concatenate([held, other], axis=0)


def local(query_features, inverse_gram, training_features, residual_weight):
    slots = lax.axis_index("z") ^ jnp.array(RELATIVE, jnp.int32)
    y = lax.axis_index("y").astype(jnp.int32)
    columns, lanes = training_features.shape
    rows, depth = inverse_gram.shape
    t = columns // NY

    folds = depth // lanes
    sent = pack(inverse_gram, training_features)
    got = lax.all_to_all(sent, "y", split_axis=0, concat_axis=0, tiled=True)
    gram_rows = got[:, :rows].reshape(NY * rows, depth)
    training = got[:, rows:].reshape(NY, t // folds, folds, lanes).transpose(2, 1, 0, 3)
    training = training.reshape(CHUNKS, 1, t // CHUNKS, NY * lanes)

    gram = lax.all_gather(gram_rows, ("x", "core"), axis=0)
    query = lax.all_gather(after(query_features, gram_rows), ("x", "core"), axis=0)
    weight = residual_weight[None, :]

    a, b = training[0], training[1]
    for distance in (4, 2, 1):
        a, b = exchange(a, distance), exchange(b, distance)
    a, b = kernel_matrix(slots, gram, a)[None], kernel_matrix(slots, gram, b)[None]
    for distance in (4, 2, 1):
        a, b = exchange(a, distance), exchange(b, distance)

    below_a, above_a = lax.ppermute(a, "y", UP), lax.ppermute(a, "y", DOWN)
    below_b, above_b = lax.ppermute(b, "y", UP), lax.ppermute(b, "y", DOWN)

    def scores(distance, chunks, out):
        return score_columns(slots, lax.rem(y + distance, NY)[None], query, chunks, weight, out)

    out = scores(0, (a, b), None)
    far = lax.ppermute(below_a, "y", UP), lax.ppermute(above_b, "y", DOWN)
    out = scores(1, (above_a, above_b), out)
    out = scores(NY - 1, (below_a, below_b), out)
    return scores(2, far, out)


def solution(mesh):
    fine = Mesh(mesh.devices.reshape(NZ, NY, 4, 2, 2), ("z", "y", "x", "core", "row"))
    pb, ta = ("z", "y"), ("x", "core")
    placed = (P(pb, ta), P(pb, ta), P(("row", *ta), pb), P(("row", *ta)))
    return jax.shard_map(
        local, mesh=fine, in_specs=placed, out_specs=P(pb, ("row", *ta)), check_vma=False
    )
```

```python
import jax
import jax.numpy as jnp
from jax import lax
from jax.experimental import pallas as pl
from jax.experimental.pallas import tpu as pltpu
from jax.sharding import Mesh, PartitionSpec as P

NZ, NY, CHUNKS = 8, 4, 2
NT_DIMS = (((1,), (1,)), ((), ()))
RELATIVE = (0, 4, 2, 6, 1, 5, 3, 7)
VMEM_LIMIT = 16 * 1024 * 1024
UP = [(i, (i + 1) % NY) for i in range(NY)]
DOWN = [(i, (i - 1) % NY) for i in range(NY)]


def pack(inverse_gram, training_features):
    rows, depth = inverse_gram.shape
    columns, lanes = training_features.shape
    t, folds = columns // NY, depth // lanes
    each = t // folds

    def kernel(gram_ref, training_ref, out_ref):
        for k in range(NY):
            out_ref[k, :rows] = gram_ref[...]
            for f in range(folds):
                first = k * t + f * each
                out_ref[k, rows:, f * lanes : (f + 1) * lanes] = training_ref[first : first + each]

    return pl.pallas_call(
        kernel,
        out_shape=jax.ShapeDtypeStruct((NY, rows + each, depth), jnp.bfloat16),
        in_specs=[pl.BlockSpec(memory_space=pltpu.VMEM)] * 2,
        out_specs=pl.BlockSpec(memory_space=pltpu.VMEM),
        compiler_params=pltpu.CompilerParams(vmem_limit_bytes=VMEM_LIMIT),
        name="pack",
    )(inverse_gram, training_features)


def kernel_matrix(slots, gram, chunks):
    n, each, depth = chunks[0].shape
    t, rows = each * len(chunks), gram.shape[1]

    def kernel(slots, gram_ref, *refs):
        chunk_refs, out_ref = refs[:-1], refs[-1]
        total = jnp.zeros((t, rows), jnp.float32)
        for s in range(n):
            block = jnp.concatenate([ref[s] for ref in chunk_refs], axis=0)
            total += lax.dot_general(block, gram_ref[slots[s]], NT_DIMS, preferred_element_type=jnp.float32)
        out_ref[...] = total.astype(out_ref.dtype)

    return pl.pallas_call(
        kernel,
        out_shape=jax.ShapeDtypeStruct((t, rows), jnp.bfloat16),
        in_specs=[pl.BlockSpec(memory_space=pltpu.SMEM)] + [pl.BlockSpec(memory_space=pltpu.VMEM)] * (1 + len(chunks)),
        out_specs=pl.BlockSpec(memory_space=pltpu.VMEM),
        compiler_params=pltpu.CompilerParams(vmem_limit_bytes=VMEM_LIMIT),
        cost_estimate=pl.CostEstimate(
            flops=2 * n * rows * t * depth, bytes_accessed=2 * n * depth * (rows + t), transcendentals=0
        ),
        name="kernel_matrix",
    )(slots, gram, *chunks)


def partial_scores(slots, query, blocks):
    _, rows, depth = query.shape
    t = blocks[0][0].shape[1]
    n = sum(array.shape[0] for array in blocks[0])
    width = t * len(blocks)
    arrays = [array for block in blocks for array in block]

    def kernel(slots, query_ref, *refs):
        array_refs, outs = list(refs[: len(arrays)]), refs[len(arrays) :]
        pieces = []
        for block in blocks:
            pieces.append([])
            for array in block:
                ref = array_refs.pop(0)
                pieces[-1].extend((ref, s) for s in range(array.shape[0]))
        for s in range(n):
            right = jnp.concatenate([piece[s][0][piece[s][1]] for piece in pieces], axis=0)
            for flip, out_ref in enumerate(outs):
                product = lax.dot_general(query_ref[slots[s] ^ flip], right, NT_DIMS, preferred_element_type=jnp.float32)
                out_ref[...] = product if s == 0 else out_ref[...] + product

    return pl.pallas_call(
        kernel,
        out_shape=[jax.ShapeDtypeStruct((rows, width), jnp.float32)] * 2,
        in_specs=[pl.BlockSpec(memory_space=pltpu.SMEM)] + [pl.BlockSpec(memory_space=pltpu.VMEM)] * (1 + len(arrays)),
        out_specs=[pl.BlockSpec(memory_space=pltpu.VMEM)] * 2,
        compiler_params=pltpu.CompilerParams(vmem_limit_bytes=VMEM_LIMIT),
        cost_estimate=pl.CostEstimate(
            flops=4 * n * rows * width * depth, bytes_accessed=2 * n * depth * (2 * rows + width), transcendentals=0
        ),
        name="partial_scores",
    )(slots, query, *arrays)


def finish(places, pairs, weight, out):
    columns = weight.shape[1]
    t = columns // NY
    rows = pairs[0][0].shape[0]
    count = places.shape[0]
    arrays = [array for pair in pairs for array in pair]

    def kernel(places, weight_ref, *refs):
        out_ref, total, sent = refs[-3:]
        sources = [(k, j) for k, pair in enumerate(pairs) for j in range(pair[0].shape[1] // t)]
        copies = []
        for p, (k, j) in enumerate(sources):
            span = pl.ds(pl.multiple_of(places[p] * t, t), t)
            mine, theirs = refs[2 * k][:, j * t : (j + 1) * t], refs[2 * k + 1][:, j * t : (j + 1) * t]
            total[p] = (mine + theirs) * weight_ref[:, span]
            copies.append(pltpu.make_async_copy(total.at[p], out_ref.at[:, span], sent.at[p]))
            copies[-1].start()
        for copy in copies:
            copy.wait()

    operands = [places, weight, *arrays]
    in_specs = [pl.BlockSpec(memory_space=pltpu.SMEM)] + [pl.BlockSpec(memory_space=pltpu.VMEM)] * (1 + len(arrays))
    aliases = {}
    if out is not None:
        in_specs.append(pl.BlockSpec(memory_space=pl.ANY))
        aliases = {len(operands): 0}
        operands.append(out)
    return pl.pallas_call(
        kernel,
        out_shape=jax.ShapeDtypeStruct((rows, columns), jnp.float32),
        in_specs=in_specs,
        out_specs=pl.BlockSpec(memory_space=pl.ANY),
        scratch_shapes=[pltpu.VMEM((count, rows, t), jnp.float32), pltpu.SemaphoreType.DMA((count,))],
        input_output_aliases=aliases,
        compiler_params=pltpu.CompilerParams(vmem_limit_bytes=VMEM_LIMIT),
        cost_estimate=pl.CostEstimate(
            flops=2 * count * rows * t, bytes_accessed=12 * count * rows * t, transcendentals=0
        ),
        name="finish",
    )(*operands)


def after(array, *earlier):
    return lax.optimization_barrier((array, earlier))[0]


def swapped(held, distance):
    return lax.ppermute(held, "z", [(i, i ^ distance) for i in range(NZ)])


def exchange(held, distance):
    return jnp.concatenate([held, swapped(held, distance)], axis=0)


def local(query_features, inverse_gram, training_features, residual_weight):
    slots = lax.axis_index("z") ^ jnp.array(RELATIVE, jnp.int32)
    ta = ("x", "core")
    columns, lanes = training_features.shape
    rows, depth = inverse_gram.shape
    t = columns // NY

    folds = depth // lanes
    sent = pack(inverse_gram, training_features)
    got = lax.all_to_all(sent, "y", split_axis=0, concat_axis=0, tiled=True)
    gram_rows = got[:, :rows].reshape(NY * rows, depth)
    training = got[:, rows:].reshape(NY, t // folds, folds, lanes).transpose(2, 1, 0, 3)
    training = training.reshape(CHUNKS, 1, t // CHUNKS, NY * lanes)

    gram = lax.all_gather(gram_rows, ta, axis=0)

    parity = [(2 * z + c, 2 * z + c if c == z % 2 else 2 * (z ^ 1) + (c ^ 1)) for z in range(NZ) for c in range(2)]
    mixed = lax.ppermute(query_features, ("z", "core"), parity)
    a, b = training[0], training[1]
    for distance in (4, 2):
        a, b = exchange(a, distance), exchange(b, distance)
    query = lax.all_gather(after(mixed, a, b), ta, axis=0)
    a, b = exchange(a, 1), exchange(b, 1)

    own = exchange(exchange(kernel_matrix(slots, gram, (a, b))[None], 4), 2)
    half = slots[: NZ // 2]
    below, above = lax.ppermute(own, "y", UP), lax.ppermute(own, "y", DOWN)
    quarter = NZ // 4
    far = lax.ppermute(below[:quarter], "y", UP), lax.ppermute(above[quarter:], "y", DOWN)

    def scores(*blocks):
        mine, other = partial_scores(half, query, blocks)
        return mine, swapped(other, 1)

    y = lax.axis_index("y").astype(jnp.int32)
    weight = residual_weight[None, :]
    places = lax.rem(y + jnp.array([0, 1, NY - 1, 2], jnp.int32), NY)
    out = finish(places[:3], (scores([own]), scores([above], [below])), weight, None)
    return finish(places[3:], (scores(far),), weight, out)


def solution(mesh):
    fine = Mesh(mesh.devices.reshape(NZ, NY, 4, 2, 2), ("z", "y", "x", "core", "row"))
    pb, ta = ("z", "y"), ("x", "core")
    placed = (P(pb, ta), P(pb, ta), P(("row", *ta), pb), P(("row", *ta)))
    return jax.shard_map(
        local, mesh=fine, in_specs=placed, out_specs=P(pb, ("row", *ta)), check_vma=False
    )
```

```python
import jax
import jax.numpy as jnp
from jax import lax
from jax.experimental import pallas as pl
from jax.experimental.pallas import tpu as pltpu
from jax.sharding import Mesh, PartitionSpec as P

NZ, NY, CHUNKS = 8, 4, 2
NT_DIMS = (((1,), (1,)), ((), ()))
RELATIVE = (0, 4, 2, 6, 1, 5, 3, 7)
VMEM_LIMIT = 16 * 1024 * 1024
UP = [(i, (i + 1) % NY) for i in range(NY)]
DOWN = [(i, (i - 1) % NY) for i in range(NY)]


def pack(inverse_gram, training_features):
    rows, depth = inverse_gram.shape
    columns, lanes = training_features.shape
    t, folds = columns // NY, depth // lanes
    each = t // folds

    def kernel(gram_ref, training_ref, out_ref):
        for k in range(NY):
            out_ref[k, :rows] = gram_ref[...]
            for f in range(folds):
                first = k * t + f * each
                out_ref[k, rows:, f * lanes : (f + 1) * lanes] = training_ref[first : first + each]

    return pl.pallas_call(
        kernel,
        out_shape=jax.ShapeDtypeStruct((NY, rows + each, depth), jnp.bfloat16),
        in_specs=[pl.BlockSpec(memory_space=pltpu.VMEM)] * 2,
        out_specs=pl.BlockSpec(memory_space=pltpu.VMEM),
        compiler_params=pltpu.CompilerParams(vmem_limit_bytes=VMEM_LIMIT),
        name="pack",
    )(inverse_gram, training_features)


def kernel_matrix(slots, gram, chunks):
    n, each, depth = chunks[0].shape
    t, rows = each * len(chunks), gram.shape[1]

    def kernel(slots, gram_ref, *refs):
        chunk_refs, out_ref = refs[:-1], refs[-1]
        total = jnp.zeros((t, rows), jnp.float32)
        for s in range(n):
            block = jnp.concatenate([ref[s] for ref in chunk_refs], axis=0)
            total += lax.dot_general(block, gram_ref[slots[s]], NT_DIMS, preferred_element_type=jnp.float32)
        out_ref[...] = total.astype(out_ref.dtype)

    return pl.pallas_call(
        kernel,
        out_shape=jax.ShapeDtypeStruct((t, rows), jnp.bfloat16),
        in_specs=[pl.BlockSpec(memory_space=pltpu.SMEM)] + [pl.BlockSpec(memory_space=pltpu.VMEM)] * (1 + len(chunks)),
        out_specs=pl.BlockSpec(memory_space=pltpu.VMEM),
        compiler_params=pltpu.CompilerParams(vmem_limit_bytes=VMEM_LIMIT),
        cost_estimate=pl.CostEstimate(
            flops=2 * n * rows * t * depth, bytes_accessed=2 * n * depth * (rows + t), transcendentals=0
        ),
        name="kernel_matrix",
    )(slots, gram, *chunks)


def partial_scores(slots, query, blocks):
    _, rows, depth = query.shape
    t = blocks[0][0].shape[1]
    n = sum(array.shape[0] for array in blocks[0])
    width = t * len(blocks)
    arrays = [array for block in blocks for array in block]

    def kernel(slots, query_ref, *refs):
        array_refs, outs = list(refs[: len(arrays)]), refs[len(arrays) :]
        pieces = []
        for block in blocks:
            pieces.append([])
            for array in block:
                ref = array_refs.pop(0)
                pieces[-1].extend((ref, s) for s in range(array.shape[0]))
        for s in range(n):
            right = jnp.concatenate([piece[s][0][piece[s][1]] for piece in pieces], axis=0)
            for flip, out_ref in enumerate(outs):
                product = lax.dot_general(query_ref[slots[s] ^ flip], right, NT_DIMS, preferred_element_type=jnp.float32)
                out_ref[...] = product if s == 0 else out_ref[...] + product

    return pl.pallas_call(
        kernel,
        out_shape=[jax.ShapeDtypeStruct((rows, width), jnp.float32)] * 2,
        in_specs=[pl.BlockSpec(memory_space=pltpu.SMEM)] + [pl.BlockSpec(memory_space=pltpu.VMEM)] * (1 + len(arrays)),
        out_specs=[pl.BlockSpec(memory_space=pltpu.VMEM)] * 2,
        compiler_params=pltpu.CompilerParams(vmem_limit_bytes=VMEM_LIMIT),
        cost_estimate=pl.CostEstimate(
            flops=4 * n * rows * width * depth, bytes_accessed=2 * n * depth * (2 * rows + width), transcendentals=0
        ),
        name="partial_scores",
    )(slots, query, *arrays)


def finish(places, pairs, weight, out):
    columns = weight.shape[1]
    t = columns // NY
    rows = pairs[0][0].shape[0]
    count = places.shape[0]
    arrays = [array for pair in pairs for array in pair]

    def kernel(places, weight_ref, *refs):
        out_ref, total, sent = refs[-3:]
        sources = [(k, j) for k, pair in enumerate(pairs) for j in range(pair[0].shape[1] // t)]
        copies = []
        for p, (k, j) in enumerate(sources):
            span = pl.ds(pl.multiple_of(places[p] * t, t), t)
            mine, theirs = refs[2 * k][:, j * t : (j + 1) * t], refs[2 * k + 1][:, j * t : (j + 1) * t]
            total[p] = (mine + theirs) * weight_ref[:, span]
            copies.append(pltpu.make_async_copy(total.at[p], out_ref.at[:, span], sent.at[p]))
            copies[-1].start()
        for copy in copies:
            copy.wait()

    operands = [places, weight, *arrays]
    in_specs = [pl.BlockSpec(memory_space=pltpu.SMEM)] + [pl.BlockSpec(memory_space=pltpu.VMEM)] * (1 + len(arrays))
    aliases = {}
    if out is not None:
        in_specs.append(pl.BlockSpec(memory_space=pl.ANY))
        aliases = {len(operands): 0}
        operands.append(out)
    return pl.pallas_call(
        kernel,
        out_shape=jax.ShapeDtypeStruct((rows, columns), jnp.float32),
        in_specs=in_specs,
        out_specs=pl.BlockSpec(memory_space=pl.ANY),
        scratch_shapes=[pltpu.VMEM((count, rows, t), jnp.float32), pltpu.SemaphoreType.DMA((count,))],
        input_output_aliases=aliases,
        compiler_params=pltpu.CompilerParams(vmem_limit_bytes=VMEM_LIMIT),
        cost_estimate=pl.CostEstimate(
            flops=2 * count * rows * t, bytes_accessed=12 * count * rows * t, transcendentals=0
        ),
        name="finish",
    )(*operands)


def after(array, *earlier):
    return lax.optimization_barrier((array, earlier))[0]


def swapped(held, distance):
    return lax.ppermute(held, "z", [(i, i ^ distance) for i in range(NZ)])


def exchange(held, distance):
    return jnp.concatenate([held, swapped(held, distance)], axis=0)


def local(query_features, inverse_gram, training_features, residual_weight):
    slots = lax.axis_index("z") ^ jnp.array(RELATIVE, jnp.int32)
    ta = ("x", "core")
    columns, lanes = training_features.shape
    rows, depth = inverse_gram.shape
    t = columns // NY

    folds = depth // lanes
    sent = pack(inverse_gram, training_features)
    got = lax.all_to_all(sent, "y", split_axis=0, concat_axis=0, tiled=True)
    gram_rows = got[:, :rows].reshape(NY * rows, depth)
    training = got[:, rows:].reshape(NY, t // folds, folds, lanes).transpose(2, 1, 0, 3)
    training = training.reshape(CHUNKS, 1, t // CHUNKS, NY * lanes)

    gram = lax.all_gather(gram_rows, ta, axis=0)

    a, b = training[0], training[1]
    for distance in (4, 2, 1):
        a, b = exchange(a, distance), exchange(b, distance)

    parity = [(2 * z + c, 2 * z + c if c == z % 2 else 2 * (z ^ 1) + (c ^ 1)) for z in range(NZ) for c in range(2)]
    mixed = lax.ppermute(after(query_features, a, b), ("z", "core"), parity)
    tile = kernel_matrix(slots, gram, (a, b))[None]
    query = lax.all_gather(after(mixed, tile), ta, axis=0)

    own = exchange(exchange(tile, 4), 2)
    half = slots[: NZ // 2]
    below, above = lax.ppermute(own, "y", UP), lax.ppermute(own, "y", DOWN)
    mine, other = partial_scores(half, query, ([own],))
    quarter = NZ // 4
    first, second = after(below[:quarter], other), after(above[quarter:], other)
    far = lax.ppermute(first, "y", UP), lax.ppermute(second, "y", DOWN)
    own_pair = mine, swapped(other, 1)

    def scores(*blocks):
        mine, other = partial_scores(half, query, blocks)
        return mine, swapped(other, 1)

    y = lax.axis_index("y").astype(jnp.int32)
    weight = residual_weight[None, :]
    places = lax.rem(y + jnp.array([0, 1, NY - 1, 2], jnp.int32), NY)
    out = finish(places[:3], (own_pair, scores([above], [below])), weight, None)
    return finish(places[3:], (scores(far),), weight, out)


def solution(mesh):
    fine = Mesh(mesh.devices.reshape(NZ, NY, 4, 2, 2), ("z", "y", "x", "core", "row"))
    pb, ta = ("z", "y"), ("x", "core")
    placed = (P(pb, ta), P(pb, ta), P(("row", *ta), pb), P(("row", *ta)))
    return jax.shard_map(
        local, mesh=fine, in_specs=placed, out_specs=P(pb, ("row", *ta)), check_vma=False
    )
```

```python
import jax
import jax.numpy as jnp
from jax import lax
from jax.experimental import pallas as pl
from jax.experimental.pallas import tpu as pltpu
from jax.sharding import Mesh, PartitionSpec as P

NZ, NY, CHUNKS = 8, 4, 2
NT_DIMS = (((1,), (1,)), ((), ()))
RELATIVE = (0, 4, 2, 6, 1, 5, 3, 7)
VMEM_LIMIT = 16 * 1024 * 1024
UP = [(i, (i + 1) % NY) for i in range(NY)]
DOWN = [(i, (i - 1) % NY) for i in range(NY)]


def pack(inverse_gram, training_features):
    rows, depth = inverse_gram.shape
    columns, lanes = training_features.shape
    t, folds = columns // NY, depth // lanes
    each = t // folds

    def kernel(gram_ref, training_ref, out_ref):
        for k in range(NY):
            out_ref[k, :rows] = gram_ref[...]
            for f in range(folds):
                first = k * t + f * each
                out_ref[k, rows:, f * lanes : (f + 1) * lanes] = training_ref[first : first + each]

    return pl.pallas_call(
        kernel,
        out_shape=jax.ShapeDtypeStruct((NY, rows + each, depth), jnp.bfloat16),
        in_specs=[pl.BlockSpec(memory_space=pltpu.VMEM)] * 2,
        out_specs=pl.BlockSpec(memory_space=pltpu.VMEM),
        compiler_params=pltpu.CompilerParams(vmem_limit_bytes=VMEM_LIMIT),
        name="pack",
    )(inverse_gram, training_features)


def kernel_matrix(slots, gram, chunks):
    n, each, depth = chunks[0].shape
    t, rows = each * len(chunks), gram.shape[1]

    def kernel(slots, gram_ref, *refs):
        chunk_refs, out_ref = refs[:-1], refs[-1]
        total = jnp.zeros((t, rows), jnp.float32)
        for s in range(n):
            block = jnp.concatenate([ref[s] for ref in chunk_refs], axis=0)
            total += lax.dot_general(block, gram_ref[slots[s]], NT_DIMS, preferred_element_type=jnp.float32)
        out_ref[...] = total.astype(out_ref.dtype)

    return pl.pallas_call(
        kernel,
        out_shape=jax.ShapeDtypeStruct((t, rows), jnp.bfloat16),
        in_specs=[pl.BlockSpec(memory_space=pltpu.SMEM)] + [pl.BlockSpec(memory_space=pltpu.VMEM)] * (1 + len(chunks)),
        out_specs=pl.BlockSpec(memory_space=pltpu.VMEM),
        compiler_params=pltpu.CompilerParams(vmem_limit_bytes=VMEM_LIMIT),
        cost_estimate=pl.CostEstimate(
            flops=2 * n * rows * t * depth, bytes_accessed=2 * n * depth * (rows + t), transcendentals=0
        ),
        name="kernel_matrix",
    )(slots, gram, *chunks)


def partial_scores(slots, query, blocks):
    _, rows, depth = query.shape
    t = blocks[0][0].shape[1]
    n = sum(array.shape[0] for array in blocks[0])
    width = t * len(blocks)
    arrays = [array for block in blocks for array in block]

    def kernel(slots, query_ref, *refs):
        array_refs, outs = list(refs[: len(arrays)]), refs[len(arrays) :]
        pieces = []
        for block in blocks:
            pieces.append([])
            for array in block:
                ref = array_refs.pop(0)
                pieces[-1].extend((ref, s) for s in range(array.shape[0]))
        for s in range(n):
            right = jnp.concatenate([piece[s][0][piece[s][1]] for piece in pieces], axis=0)
            for flip, out_ref in enumerate(outs):
                product = lax.dot_general(query_ref[slots[s] ^ flip], right, NT_DIMS, preferred_element_type=jnp.float32)
                out_ref[...] = product if s == 0 else out_ref[...] + product

    return pl.pallas_call(
        kernel,
        out_shape=[jax.ShapeDtypeStruct((rows, width), jnp.float32)] * 2,
        in_specs=[pl.BlockSpec(memory_space=pltpu.SMEM)] + [pl.BlockSpec(memory_space=pltpu.VMEM)] * (1 + len(arrays)),
        out_specs=[pl.BlockSpec(memory_space=pltpu.VMEM)] * 2,
        compiler_params=pltpu.CompilerParams(vmem_limit_bytes=VMEM_LIMIT),
        cost_estimate=pl.CostEstimate(
            flops=4 * n * rows * width * depth, bytes_accessed=2 * n * depth * (2 * rows + width), transcendentals=0
        ),
        name="partial_scores",
    )(slots, query, *arrays)


def finish(places, pairs, weight, out):
    columns = weight.shape[1]
    t = columns // NY
    rows = pairs[0][0].shape[0]
    count = places.shape[0]
    arrays = [array for pair in pairs for array in pair]

    def kernel(places, weight_ref, *refs):
        out_ref, total, sent = refs[-3:]
        sources = [(k, j) for k, pair in enumerate(pairs) for j in range(pair[0].shape[1] // t)]
        copies = []
        for p, (k, j) in enumerate(sources):
            span = pl.ds(pl.multiple_of(places[p] * t, t), t)
            mine, theirs = refs[2 * k][:, j * t : (j + 1) * t], refs[2 * k + 1][:, j * t : (j + 1) * t]
            total[p] = (mine + theirs) * weight_ref[:, span]
            copies.append(pltpu.make_async_copy(total.at[p], out_ref.at[:, span], sent.at[p]))
            copies[-1].start()
        for copy in copies:
            copy.wait()

    operands = [places, weight, *arrays]
    in_specs = [pl.BlockSpec(memory_space=pltpu.SMEM)] + [pl.BlockSpec(memory_space=pltpu.VMEM)] * (1 + len(arrays))
    aliases = {}
    if out is not None:
        in_specs.append(pl.BlockSpec(memory_space=pl.ANY))
        aliases = {len(operands): 0}
        operands.append(out)
    return pl.pallas_call(
        kernel,
        out_shape=jax.ShapeDtypeStruct((rows, columns), jnp.float32),
        in_specs=in_specs,
        out_specs=pl.BlockSpec(memory_space=pl.ANY),
        scratch_shapes=[pltpu.VMEM((count, rows, t), jnp.float32), pltpu.SemaphoreType.DMA((count,))],
        input_output_aliases=aliases,
        compiler_params=pltpu.CompilerParams(vmem_limit_bytes=VMEM_LIMIT),
        cost_estimate=pl.CostEstimate(
            flops=2 * count * rows * t, bytes_accessed=12 * count * rows * t, transcendentals=0
        ),
        name="finish",
    )(*operands)


def after(array, *earlier):
    return lax.optimization_barrier((array, earlier))[0]


def swapped(held, distance):
    return lax.ppermute(held, "z", [(i, i ^ distance) for i in range(NZ)])


def exchange(held, distance):
    return jnp.concatenate([held, swapped(held, distance)], axis=0)


def local(query_features, inverse_gram, training_features, residual_weight):
    slots = lax.axis_index("z") ^ jnp.array(RELATIVE, jnp.int32)
    ta = ("x", "core")
    columns, lanes = training_features.shape
    rows, depth = inverse_gram.shape
    t = columns // NY

    folds = depth // lanes
    parity = [(2 * z + c, 2 * z + c if c == z % 2 else 2 * (z ^ 1) + (c ^ 1)) for z in range(NZ) for c in range(2)]
    mixed = lax.ppermute(query_features, ("z", "core"), parity)
    sent = after(pack(inverse_gram, training_features), mixed)
    got = lax.all_to_all(sent, "y", split_axis=0, concat_axis=0, tiled=True)
    gram_rows = got[:, :rows].reshape(NY * rows, depth)
    training = got[:, rows:].reshape(NY, t // folds, folds, lanes).transpose(2, 1, 0, 3)
    training = training.reshape(CHUNKS, 1, t // CHUNKS, NY * lanes)

    gram = lax.all_gather(gram_rows, ta, axis=0)

    a, b = training[0], training[1]
    for distance in (4, 2):
        a, b = exchange(a, distance), exchange(b, distance)
    query = lax.all_gather(after(mixed, a, b), ta, axis=0)
    a, b = exchange(a, 1), exchange(b, 1)

    own = exchange(exchange(kernel_matrix(slots, gram, (a, b))[None], 4), 2)
    half = slots[: NZ // 2]
    own = after(own, query)
    below, above = lax.ppermute(own, "y", UP), lax.ppermute(own, "y", DOWN)
    mine, other = partial_scores(half, query, ([own],))
    own_pair = mine, swapped(other, 1)
    quarter = NZ // 4
    first, second = after(below[:quarter], other), after(above[quarter:], other)
    far = lax.ppermute(first, "y", UP), lax.ppermute(second, "y", DOWN)

    def scores(*blocks):
        mine, other = partial_scores(half, query, blocks)
        return mine, swapped(other, 1)

    y = lax.axis_index("y").astype(jnp.int32)
    weight = residual_weight[None, :]
    places = lax.rem(y + jnp.array([0, 1, NY - 1, 2], jnp.int32), NY)
    out = finish(places[:3], (own_pair, scores([after(above, own_pair[1])], [below])), weight, None)
    return finish(places[3:], (scores(far),), weight, out)


def solution(mesh):
    fine = Mesh(mesh.devices.reshape(NZ, NY, 4, 2, 2), ("z", "y", "x", "core", "row"))
    pb, ta = ("z", "y"), ("x", "core")
    placed = (P(pb, ta), P(pb, ta), P(("row", *ta), pb), P(("row", *ta)))
    return jax.shard_map(
        local, mesh=fine, in_specs=placed, out_specs=P(pb, ("row", *ta)), check_vma=False
    )
```

```python
import jax
import jax.numpy as jnp
from jax import lax
from jax.experimental import pallas as pl
from jax.experimental.pallas import tpu as pltpu
from jax.sharding import Mesh, PartitionSpec as P

NZ, NY = 8, 4
NT_DIMS = (((1,), (1,)), ((), ()))
RELATIVE = (0, 4, 2, 6, 1, 5, 3, 7)
VMEM_LIMIT = 16 * 1024 * 1024
UP = [(i, (i + 1) % NY) for i in range(NY)]
DOWN = [(i, (i - 1) % NY) for i in range(NY)]


def pack(inverse_gram, training_features):
    rows, depth = inverse_gram.shape
    columns, lanes = training_features.shape
    t, folds = columns // NY, depth // lanes
    each = t // folds

    def kernel(gram_ref, training_ref, out_ref):
        for k in range(NY):
            out_ref[k, :rows] = gram_ref[...]
            for f in range(folds):
                first = k * t + f * each
                out_ref[k, rows:, f * lanes : (f + 1) * lanes] = training_ref[first : first + each]

    return pl.pallas_call(
        kernel,
        out_shape=jax.ShapeDtypeStruct((NY, rows + each, depth), jnp.bfloat16),
        in_specs=[pl.BlockSpec(memory_space=pltpu.VMEM)] * 2,
        out_specs=pl.BlockSpec(memory_space=pltpu.VMEM),
        compiler_params=pltpu.CompilerParams(vmem_limit_bytes=VMEM_LIMIT),
        name="pack",
    )(inverse_gram, training_features)


def kernel_matrix(slots, gram, training):
    n, t, depth = training.shape
    rows = gram.shape[1]

    def kernel(slots, gram_ref, training_ref, out_ref):
        total = jnp.zeros((t, rows), jnp.float32)
        for s in range(n):
            total += lax.dot_general(training_ref[s], gram_ref[slots[s]], NT_DIMS, preferred_element_type=jnp.float32)
        out_ref[...] = total.astype(out_ref.dtype)

    return pl.pallas_call(
        kernel,
        out_shape=jax.ShapeDtypeStruct((t, rows), jnp.bfloat16),
        in_specs=[pl.BlockSpec(memory_space=pltpu.SMEM)] + [pl.BlockSpec(memory_space=pltpu.VMEM)] * 2,
        out_specs=pl.BlockSpec(memory_space=pltpu.VMEM),
        compiler_params=pltpu.CompilerParams(vmem_limit_bytes=VMEM_LIMIT),
        cost_estimate=pl.CostEstimate(
            flops=2 * n * rows * t * depth, bytes_accessed=2 * n * depth * (rows + t), transcendentals=0
        ),
        name="kernel_matrix",
    )(slots, gram, training)


def score_columns(slots, place, query, chunks, weight, out):
    n, rows, depth = query.shape
    t = sum(chunk.shape[1] for chunk in chunks)
    columns = weight.shape[1]

    def kernel(slots, place, query_ref, weight_ref, *refs):
        chunk_refs = refs[: len(chunks)]
        out_ref, total, sent = refs[-3:]
        span = pl.ds(pl.multiple_of(place[0] * t, t), t)
        for s in range(n):
            block = jnp.concatenate([ref[s] for ref in chunk_refs], axis=0)
            product = lax.dot_general(query_ref[slots[s]], block, NT_DIMS, preferred_element_type=jnp.float32)
            if s == 0:
                total[...] = product
            elif s < n - 1:
                total[...] += product
            else:
                total[...] = (total[...] + product) * weight_ref[:, span]
        copy = pltpu.make_async_copy(total, out_ref.at[:, span], sent)
        copy.start()
        copy.wait()

    operands = [slots, place, query, weight, *chunks]
    in_specs = [pl.BlockSpec(memory_space=pltpu.SMEM)] * 2 + [pl.BlockSpec(memory_space=pltpu.VMEM)] * (2 + len(chunks))
    aliases = {}
    if out is not None:
        in_specs.append(pl.BlockSpec(memory_space=pl.ANY))
        aliases = {len(operands): 0}
        operands.append(out)
    return pl.pallas_call(
        kernel,
        out_shape=jax.ShapeDtypeStruct((rows, columns), jnp.float32),
        in_specs=in_specs,
        out_specs=pl.BlockSpec(memory_space=pl.ANY),
        scratch_shapes=[pltpu.VMEM((rows, t), jnp.float32), pltpu.SemaphoreType.DMA],
        input_output_aliases=aliases,
        compiler_params=pltpu.CompilerParams(vmem_limit_bytes=VMEM_LIMIT),
        cost_estimate=pl.CostEstimate(
            flops=2 * n * rows * t * depth, bytes_accessed=2 * n * depth * (rows + t), transcendentals=0
        ),
        name="score_columns",
    )(*operands)


def after(array, *earlier):
    return lax.optimization_barrier((array, earlier))[0]


def exchange(held, distance):
    other = lax.ppermute(held, "z", [(i, i ^ distance) for i in range(NZ)])
    return jnp.concatenate([held, other], axis=0)


def local(query_features, inverse_gram, training_features, residual_weight):
    slots = lax.axis_index("z") ^ jnp.array(RELATIVE, jnp.int32)
    y = lax.axis_index("y").astype(jnp.int32)
    columns, lanes = training_features.shape
    rows, depth = inverse_gram.shape
    t = columns // NY

    folds = depth // lanes
    sent = pack(inverse_gram, training_features)
    got = lax.all_to_all(sent, "y", split_axis=0, concat_axis=0, tiled=True)
    gram_rows = got[:, :rows].reshape(NY * rows, depth)
    training = got[:, rows:].reshape(NY, t // folds, folds, lanes).transpose(2, 1, 0, 3)
    training = training.reshape(1, t, NY * lanes)

    gram = lax.all_gather(gram_rows, ("x", "core"), axis=0)
    query = lax.all_gather(after(query_features, gram_rows), ("x", "core"), axis=0)
    weight = residual_weight[None, :]

    a, b = training[:, : 3 * t // 8], training[:, 3 * t // 8 :]
    for distance in (4, 2, 1):
        a, b = exchange(a, distance), exchange(b, distance)
    a, b = kernel_matrix(slots, gram, a)[None], kernel_matrix(slots, gram, b)[None]
    for distance in (4, 2, 1):
        a, b = exchange(a, distance), exchange(b, distance)

    below_a, above_a = lax.ppermute(a, "y", UP), lax.ppermute(a, "y", DOWN)
    below_b, above_b = lax.ppermute(b, "y", UP), lax.ppermute(b, "y", DOWN)

    def scores(distance, chunks, out):
        return score_columns(slots, lax.rem(y + distance, NY)[None], query, chunks, weight, out)

    out = scores(0, (a, b), None)
    far = lax.ppermute(below_a, "y", UP), lax.ppermute(above_b, "y", DOWN)
    out = scores(1, (above_a, above_b), out)
    out = scores(NY - 1, (below_a, below_b), out)
    return scores(2, far, out)


def solution(mesh):
    fine = Mesh(mesh.devices.reshape(NZ, NY, 4, 2, 2), ("z", "y", "x", "core", "row"))
    pb, ta = ("z", "y"), ("x", "core")
    placed = (P(pb, ta), P(pb, ta), P(("row", *ta), pb), P(("row", *ta)))
    return jax.shard_map(
        local, mesh=fine, in_specs=placed, out_specs=P(pb, ("row", *ta)), check_vma=False
    )
```
